128 devices in a mesh: dom: 32 (over y, x, core), mode: 4 (over z).
Axes of the slice: x: 4, y: 4, z: 4, core: 2. Of those that a mesh axis runs over, the one named last changes fastest.
Arguments:
- mode_shapes: bfloat16 [128, 6, 32768], P('mode', None, 'dom'), may hold values from -0.29882812 to 0.29882812
- eigenvalues: float32 [128], replicated, may hold values from 0.7 to 192, as said below
- mode_weights: float32 [128], P('mode'), may hold values from 0.1 to 1
- stiff_deriv: bfloat16 [24, 24, 49152], P(None, None, 'dom'), as said below
- mass_ref: bfloat16 [24, 24], replicated, as said below
- mass_scale: float32 [49152], P('dom'), may hold values from 0.5 to 2
- connectivity: int32 [4, 49152], P(None, 'dom'), may hold values from 0 to 1087, as said below
- design_owner: int32 [49152], P('dom'), may hold values from 0 to 20479, as said below
- direction: float32 [20480], P('dom'), may hold values from -0.12 to 0.12
Outputs:
- hess_vec: float32 [20480], P('dom')
- eig_deriv: float32 [128], P('mode')
The draws below stay inside these ranges and needn't reach their ends.
Inputs may be any that keep to these rules, and one draw needn't show every extreme that they name: Distinct eigenvalues, increasing with the mode index, neighbours at least 0.4 apart. `stiff_deriv`: symmetric 24 by 24 matrices with a positive diagonal. `mass_ref`: Symmetric, with a positive diagonal. `connectivity`: index into the extended node list of the element's device: the 32 upper rim nodes of the lower neighbour, the device's own 1024 nodes, then the 32 lower rim nodes of the upper neighbour. The corners of one element lie within 64 positions of one another. Elements of the first device never name the lower rim; those of the last never name the upper rim. `design_owner`: an element of index r of dom has its design variable in the blocks of 640 design variables of indices r - 1, r or r + 1 of dom.
All inputs are finite; a program needn't handle non-finite values.
Results may differ from the reference program's by a relative error of at most 0.01.
Values may be sent and summed in bfloat16 or wider, within the bound.
No kernel may reach another device: no remote copies, remote signals or barrier semaphores. Data moves between devices by JAX's collectives and lax.ppermute only.
A program may use at most 64 MiB of HBM per device.

```python
import math
import jax
import jax.numpy as jnp
from jax import lax

MODES = 128
DESIGNS = 20480
NODE_DEV = 1024
ELEM_DEV = 1536
H = 32
NODES = 32768
ELEMS = 49152
DES_DEV = 640
N_DOM = 32


def draw_eigenvalues(key, part):
    ranks = jnp.arange(MODES, dtype=jnp.float32)
    jitter = jax.random.uniform(key, (MODES,), jnp.float32, -0.3, 0.3)
    return 1.0 + ranks + jitter


def draw_stiff_deriv(key, part):
    noise = jax.random.normal(key, (24, 24, ELEMS), jnp.float32)
    matrix = (noise + jnp.transpose(noise, (1, 0, 2))) * 0.25 + 3.0 * jnp.eye(24, dtype=jnp.float32)[:, :, None]
    return matrix.astype(jnp.bfloat16)


def draw_mass_ref(key, part):
    noise = jax.random.uniform(key, (24, 24), jnp.float32, -0.3, 0.3)
    matrix = (noise + noise.T) * 0.5 + 2.0 * jnp.eye(24, dtype=jnp.float32)
    return matrix.astype(jnp.bfloat16)


def draw_connectivity(key, part):
    owner_rank = jnp.arange(ELEMS, dtype=jnp.int32) // ELEM_DEV
    position = jnp.arange(ELEMS, dtype=jnp.int32) % ELEM_DEV
    lower = jnp.where(owner_rank == 0, H, 0).astype(jnp.int32)
    upper = jnp.where(owner_rank == N_DOM - 1, NODE_DEV + H - 1, NODE_DEV + 2 * H - 1).astype(jnp.int32)
    center_key = jax.random.fold_in(key, 21)
    offset_key = jax.random.fold_in(key, 23)
    center = jax.random.randint(center_key, (ELEMS,), H, H + NODE_DEV).astype(jnp.int32)
    offset = jax.random.randint(offset_key, (4, ELEMS), -H, H + 1).astype(jnp.int32)
    corners = jnp.clip(center[None, :] + offset, lower[None, :], upper[None, :])
    corner_rank = jnp.arange(4, dtype=jnp.int32)[:, None]
    low_edge = lower[None, :] + corner_rank
    high_edge = upper[None, :] - corner_rank
    corners = jnp.where(position[None, :] == 0, low_edge, corners)
    corners = jnp.where(position[None, :] == 1, high_edge, corners)
    return corners.astype(jnp.int32)


def draw_design_owner(key, part):
    owner_rank = jnp.arange(ELEMS, dtype=jnp.int32) // ELEM_DEV
    first_key = jax.random.fold_in(key, 11)
    second_key = jax.random.fold_in(key, 13)
    step_off = jax.random.randint(first_key, (ELEMS,), -1, 2).astype(jnp.int32)
    block = jnp.clip(owner_rank + step_off, 0, N_DOM - 1)
    within = jax.random.randint(second_key, (ELEMS,), 0, DES_DEV).astype(jnp.int32)
    return (block * DES_DEV + within).astype(jnp.int32)


def level_of(key, dims, shards, smallest, largest):
    def one(dim, blocks):
        draws = jax.random.uniform(jax.random.fold_in(jax.random.fold_in(key, 6), dim), (blocks,), jnp.float32, smallest / len(shards), largest / len(shards))
        return jnp.repeat(jnp.exp(draws), dims[dim] // blocks).reshape((-1,) + (1,) * (len(dims) - dim - 1))

    loudness = one(*shards[0])
    for cut in shards[1:]:
        loudness = loudness * one(*cut)
    return loudness


def scatter_about(key, dims, scale, limit, pieces=(), kind=jnp.bfloat16):
    result = jax.random.normal(key, dims, jnp.float32) * scale
    if len(pieces) > 0:
        result = level_of(key, dims, pieces, -0.22, 0.18) * result
    return jnp.clip(result, min=-limit, max=limit).astype(kind)


def setup_inputs(seed: int = 0) -> dict:
    seeds = jax.random.split(jax.random.key(seed), 10)
    mode_shapes = scatter_about(seeds[0], (MODES, 6, NODES), 0.05, 0.29882812, ((0, 4), (2, 32)))
    eigenvalues = draw_eigenvalues(jax.random.fold_in(seeds[9], 71), 0)
    mode_weights = jnp.clip(jnp.exp(math.log(1.0) - 2.3025851 * jax.random.uniform(seeds[2], (MODES,), jnp.float32) ** level_of(seeds[2], (MODES,), ((0, 4),), -0.2, 0.2)), 0.1, 1.0)
    stiff_deriv = draw_stiff_deriv(jax.random.fold_in(seeds[9], 71), 0)
    mass_ref = draw_mass_ref(jax.random.fold_in(seeds[9], 71), 0)
    mass_scale = jnp.clip(jnp.exp(math.log(2.0) - 1.3862944 * jax.random.uniform(seeds[5], (ELEMS,), jnp.float32) ** level_of(seeds[5], (ELEMS,), ((0, 32),), -0.2, 0.2)), 0.5, 2.0)
    connectivity = draw_connectivity(jax.random.fold_in(seeds[9], 71), 0)
    design_owner = draw_design_owner(jax.random.fold_in(seeds[9], 71), 0)
    direction = scatter_about(seeds[8], (DESIGNS,), 0.02, 0.12, ((0, 32),), jnp.float32)
    return {"mode_shapes": mode_shapes, "eigenvalues": eigenvalues, "mode_weights": mode_weights, "stiff_deriv": stiff_deriv, "mass_ref": mass_ref, "mass_scale": mass_scale, "connectivity": connectivity, "design_owner": design_owner, "direction": direction}


HIGH = lax.Precision.HIGHEST


def element_dofs(field, element_nodes):
    picked = field[:, :, element_nodes]
    return picked.reshape(field.shape[0], 24, element_nodes.shape[1])


def reference(mode_shapes, eigenvalues, mode_weights, stiff_deriv, mass_ref, mass_scale, connectivity, design_owner, direction):
    padded = jnp.pad(mode_shapes, ((0, 0), (0, 0), (H, H)))
    deriv_elem = direction[design_owner]
    offsets = jnp.arange(N_DOM, dtype=jnp.int32) * NODE_DEV
    nodes_split = jnp.moveaxis(connectivity.reshape(4, N_DOM, ELEM_DEV), 1, 0) + offsets[:, None, None]
    stiff_split = jnp.moveaxis(stiff_deriv.reshape(24, 24, N_DOM, ELEM_DEV), 2, 0)
    dir_split = deriv_elem.reshape(N_DOM, ELEM_DEV)
    mass_split = mass_scale.reshape(N_DOM, ELEM_DEV)
    mass_wide = mass_ref.astype(jnp.float32)

    def gram_step(totals, slices):
        element_nodes, matrices, elem_dir, elem_mass = slices
        shapes = element_dofs(padded, element_nodes).astype(jnp.float32)
        stiff_part = jnp.einsum('abe,mbe->mae', matrices.astype(jnp.float32), shapes, precision=HIGH)
        force_k = (elem_dir * stiff_part).astype(jnp.bfloat16).astype(jnp.float32)
        mass_shapes = jnp.einsum('ab,mbe->mae', mass_wide, shapes, precision=HIGH)
        force_m = (elem_dir * elem_mass * mass_shapes).astype(jnp.bfloat16).astype(jnp.float32)
        stiff_gram = jnp.einsum('jae,iae->ji', shapes, force_k, precision=HIGH)
        mass_gram = jnp.einsum('jae,iae->ji', shapes, force_m, precision=HIGH)
        return (totals[0] + stiff_gram, totals[1] + mass_gram), None

    empty = jnp.zeros((MODES, MODES), jnp.float32)
    (stiff_gram, mass_gram), unused = lax.scan(gram_step, (empty, empty), (nodes_split, stiff_split, dir_split, mass_split))
    resid = stiff_gram - eigenvalues[None, :] * mass_gram
    eig_deriv = jnp.diagonal(resid)
    diagonal_mask = jnp.eye(MODES, dtype=bool)
    spacing = eigenvalues[None, :] - eigenvalues[:, None]
    combiner = jnp.where(diagonal_mask, -0.5 * jnp.diagonal(mass_gram)[None, :], resid / jnp.where(diagonal_mask, 1.0, spacing)).astype(jnp.bfloat16)
    shape_deriv = jnp.einsum('ji,jcn->icn', combiner.astype(jnp.float32), mode_shapes.astype(jnp.float32), precision=HIGH).astype(jnp.bfloat16)
    deriv_pad = jnp.pad(shape_deriv, ((0, 0), (0, 0), (H, H)))

    def energy_step(unused_carry, slices):
        element_nodes, matrices, elem_mass = slices
        shapes = element_dofs(padded, element_nodes).astype(jnp.float32)
        deriv_dofs = element_dofs(deriv_pad, element_nodes).astype(jnp.float32)
        stiff_q = jnp.einsum('abe,mbe->mae', matrices.astype(jnp.float32), deriv_dofs, precision=HIGH)
        mass_q = jnp.einsum('ab,mbe->mae', mass_wide, deriv_dofs, precision=HIGH)
        mass_shapes = jnp.einsum('ab,mbe->mae', mass_wide, shapes, precision=HIGH)
        term_k = jnp.sum(shapes * stiff_q, axis=1)
        term_m = jnp.sum(shapes * mass_q, axis=1)
        term_p = jnp.sum(shapes * mass_shapes, axis=1)
        inner = 2.0 * term_k - elem_mass[None, :] * (2.0 * eigenvalues[:, None] * term_m + eig_deriv[:, None] * term_p)
        return unused_carry, jnp.sum(mode_weights[:, None] * inner, axis=0)

    unused2, energy = lax.scan(energy_step, 0.0, (nodes_split, stiff_split, mass_split))
    hess_vec = jax.ops.segment_sum(energy.reshape(-1), design_owner, num_segments=DESIGNS)
    return hess_vec, eig_deriv
```

```python
import functools

import jax
import jax.numpy as jnp
from jax import lax
from jax.experimental import pallas as pl
from jax.experimental.pallas import tpu as pltpu
from jax.sharding import PartitionSpec as P

H = 32
COMPS = 6
CORNERS = 4
DOFS = 24
TILE = 256
LANES = 128
MIB = 1 << 20
f32, bf16 = jnp.float32, jnp.bfloat16


def dot(a, b):
    return lax.dot_general(a, b, (((1,), (0,)), ((), ())), preferred_element_type=f32)


def dot_nt(a, b):
    return lax.dot_general(a, b, (((1,), (1,)), ((), ())), preferred_element_type=f32)


def iota(shape, dim):
    return lax.broadcasted_iota(jnp.int32, shape, dim)


def one_hot(rows, index):
    hit = iota((rows, index.shape[1]), 0) == index
    return jnp.where(hit, 1.0, 0.0).astype(bf16)


def three_pieces(x):
    first = x.astype(bf16)
    rest = x - first.astype(f32)
    second = rest.astype(bf16)
    third = (rest - second.astype(f32)).astype(bf16)
    return first, second, third


def column_of(row, offset, count):
    n = row.shape[1]
    mask = iota((count, n), 1) == iota((count, n), 0) + offset
    return jnp.sum(jnp.where(mask, row, 0.0), axis=1, keepdims=True)


def fill_one_hot(conn_ref, own_hot, rim_hot, nodes):
    for k in range(CORNERS):
        index = conn_ref[k : k + 1, :]
        cols = pl.ds(k * TILE, TILE)
        own_hot[:, cols] = one_hot(nodes, index - H)
        rim = jnp.where(index < H, index, jnp.where(index < nodes + H, -1, index - nodes))
        rim_hot[:, cols] = one_hot(2 * H, rim)


def forces_kernel(
    modes,
    nodes,
    des,
    conn_ref,
    owner_ref,
    mass_ref_,
    stiff_ref,
    field_ref,
    rim_ref,
    dir_low_ref,
    dir_own_ref,
    dir_high_ref,
    ref_ref,
    eig_ref,
    weight_ref,
    resid_ref,
    power_ref,
    node_ref,
    node_rim_ref,
    diag_ref,
    mass_big,
    table,
    own_hot,
    rim_hot,
    shapes,
    stacked,
    mass_q,
    stiff_wide,
    force,
):
    step = pl.program_id(0)
    rows = COMPS * modes
    big = CORNERS * rows
    rank = lax.axis_index("dom")
    mode_start = lax.axis_index("mode") * modes

    @pl.when(step == 0)
    def _():
        row = iota((big, DOFS), 0)
        dof = CORNERS * ((row % rows) // modes) + row // rows
        spread = jnp.where(dof == iota((big, DOFS), 1), 1.0, 0.0).astype(bf16)
        half = dot(spread, ref_ref[...]).astype(bf16)
        for part in range(CORNERS):
            span = pl.ds(part * rows, rows)
            wide = dot_nt(half, spread[part * rows : (part + 1) * rows])
            same = iota((big, rows), 0) % modes == iota((big, rows), 1) % modes
            mass_big[:, span] = jnp.where(same, wide, 0.0).astype(bf16)
        per = des // LANES
        table[...] = jnp.zeros_like(table)
        for side, ref in enumerate((dir_low_ref, dir_own_ref, dir_high_ref)):
            for i in range(per):
                at = side * per + i
                table[at : at + 1, :] = ref[:, i * LANES : (i + 1) * LANES]
        node_ref[...] = jnp.zeros_like(node_ref)
        node_rim_ref[...] = jnp.zeros_like(node_rim_ref)
        diag_ref[...] = jnp.zeros_like(diag_ref)

    eig = column_of(eig_ref[...], mode_start, modes)
    weight = 2.0 * column_of(weight_ref[...], 0, modes)

    local = owner_ref[...] - (rank - 1) * des
    entries = table.shape[0]
    pieces = jnp.concatenate(three_pieces(table[...]), axis=0)
    looked = dot(pieces, one_hot(LANES, local % LANES))
    looked = looked[:entries] + looked[entries : 2 * entries] + looked[2 * entries :]
    here = iota((entries, TILE), 0) == local // LANES
    elem_dir = jnp.sum(jnp.where(here, looked, 0.0), axis=0, keepdims=True)
    elem_mass = mass_ref_[...]

    fill_one_hot(conn_ref, own_hot, rim_hot, nodes)
    shapes[...] = dot(field_ref[...], own_hot[...]) + dot(rim_ref[...], rim_hot[...])
    for k in range(CORNERS):
        stacked[k * rows : (k + 1) * rows, :] = shapes[:, k * TILE : (k + 1) * TILE].astype(bf16)
    mass_q[...] = dot(mass_big[...], stacked[...])
    stiff_wide[...] = stiff_ref[...].astype(f32)

    for lane in range(TILE // LANES):
        cols = slice(lane * LANES, (lane + 1) * LANES)
        direction = elem_dir[:, cols]
        mass = elem_mass[:, cols]
        scaled = eig * mass
        power = jnp.zeros((modes, LANES), f32)
        for first in range(0, DOFS, 4):
            sums = [jnp.zeros((modes, LANES), f32) for _ in range(4)]
            for b in range(DOFS):
                c, k = b // CORNERS, b % CORNERS
                at = k * TILE + lane * LANES
                s = shapes[c * modes : (c + 1) * modes, at : at + LANES]
                for q in range(4):
                    sums[q] = sums[q] + stiff_wide[first + q, b : b + 1, cols] * s
            for q in range(4):
                c, k = (first + q) // CORNERS, (first + q) % CORNERS
                at = k * TILE + lane * LANES
                s = shapes[c * modes : (c + 1) * modes, at : at + LANES]
                base = k * rows + c * modes
                mq = mass_q[base : base + modes, cols]
                power = power + s * mq
                resid = sums[q] - scaled * mq
                force[c * modes : (c + 1) * modes, at : at + LANES] = (direction * resid).astype(bf16)
                resid_ref[base : base + modes, cols] = weight * resid
        power = power * mass
        power_ref[:, cols] = power
        diag_ref[...] += direction * power

    node_ref[...] += dot_nt(force[...], own_hot[...])
    node_rim_ref[...] += dot_nt(force[...], rim_hot[...])


def gather_modes(refs, c, modes):
    return jnp.concatenate([r[c * modes : (c + 1) * modes, :] for r in refs], axis=0)


def gram_kernel(modes, groups, node_ref, node_rim_ref, diag_ref, *rest):
    fields, rims, out_ref = rest[:groups], rest[groups : 2 * groups], rest[2 * groups]
    total = jnp.zeros((modes, groups * modes), f32)
    for c in range(COMPS):
        span = slice(c * modes, (c + 1) * modes)
        for part, parts in ((node_ref, fields), (node_rim_ref, rims)):
            exact = part[span, :]
            high = exact.astype(bf16)
            low = (exact - high.astype(f32)).astype(bf16)
            both = dot_nt(jnp.concatenate([high, low], axis=0), gather_modes(parts, c, modes))
            total = total + both[:modes] + both[modes:]
    out_ref[0:modes, :] = total
    diag = jnp.sum(diag_ref[...], axis=1, keepdims=True)
    mask = iota((modes, LANES), 0) == iota((modes, LANES), 1)
    out_ref[modes : modes + 8, :] = jnp.broadcast_to(
        jnp.sum(jnp.where(mask, diag, 0.0), axis=0, keepdims=True), (8, LANES)
    )


def energy_kernel(modes, groups, nodes, des, parts, *refs):
    gram_refs, refs = refs[:parts], refs[parts:]
    eig_ref, weight_ref = refs[:2]
    fields, rims, refs = refs[2 : 2 + groups], refs[2 + groups : 2 + 2 * groups], refs[2 + 2 * groups :]
    conn_ref, owner_ref, resid_ref, power_ref = refs[:4]
    low_ref, own_ref, high_ref, deriv_ref = refs[4:8]
    deriv, deriv_rim, factor, own_hot, rim_hot, totals = refs[8:]
    step = pl.program_id(0)
    rows = COMPS * modes
    rank = lax.axis_index("dom")
    mode_start = lax.axis_index("mode") * modes

    @pl.when(step == 0)
    def _():
        total = gram_refs[0][...]
        for ref in gram_refs[1:]:
            total = total + ref[...]
        gram = total[:modes]
        mass_diag = total[modes : modes + 1]
        shape = (modes, groups * modes)
        mask = iota(shape, 0) == iota(shape, 1)
        eig_rows = jnp.broadcast_to(eig_ref[...], (8, LANES))
        turned = pltpu.roll(eig_rows, lax.rem(LANES - mode_start, LANES), 1)[0:1]
        spacing = column_of(turned, 0, modes) - turned
        combiner = jnp.where(
            mask, -0.5 * mass_diag, gram / jnp.where(mask, 1.0, spacing)
        ).astype(bf16)
        diagonal = jnp.where(mask, gram, 0.0)
        deriv_ref[...] = jnp.sum(diagonal, axis=0, keepdims=True)[:, :modes]
        eig_deriv = jnp.sum(diagonal, axis=1, keepdims=True)
        factor[...] = jnp.broadcast_to(
            eig_deriv * column_of(weight_ref[...], 0, modes), factor.shape
        )
        for c in range(COMPS):
            span = slice(c * modes, (c + 1) * modes)
            deriv[span, :] = dot(combiner, gather_modes(fields, c, modes)).astype(bf16)
            deriv_rim[span, :] = dot(combiner, gather_modes(rims, c, modes)).astype(bf16)
        totals[...] = jnp.zeros_like(totals)

    fill_one_hot(conn_ref, own_hot, rim_hot, nodes)
    moved = dot(deriv[...], own_hot[...]) + dot(deriv_rim[...], rim_hot[...])
    energies = []
    for lane in range(TILE // LANES):
        cols = slice(lane * LANES, (lane + 1) * LANES)
        total = -factor[...] * power_ref[:, cols]
        for k in range(CORNERS):
            at = k * TILE + lane * LANES
            for c in range(COMPS):
                base = k * rows + c * modes
                total = total + moved[c * modes : (c + 1) * modes, at : at + LANES] * resid_ref[
                    base : base + modes, cols
                ]
        energies.append(jnp.sum(total, axis=0, keepdims=True))
    energy = jnp.concatenate(energies, axis=1)
    local = owner_ref[...] - (rank - 1) * des
    entries = totals.shape[0]
    here = iota((entries, TILE), 0) == local // LANES
    spread = jnp.concatenate(
        [jnp.where(here, p.astype(f32), 0.0).astype(bf16) for p in three_pieces(energy)], axis=0
    )
    sums = dot_nt(spread, one_hot(LANES, local % LANES))
    totals[...] += sums[:entries] + sums[entries : 2 * entries] + sums[2 * entries :]

    @pl.when(step == pl.num_programs(0) - 1)
    def _():
        per = des // LANES
        for side, ref in enumerate((low_ref, own_ref, high_ref)):
            for i in range(per):
                at = side * per + i
                ref[:, i * LANES : (i + 1) * LANES] = totals[at : at + 1, :]


def shift_in(value, axis, step):
    count = lax.axis_size(axis)
    return lax.ppermute(value, axis, [(i, (i - step) % count) for i in range(count)])


def neighbour(value, step):
    count = lax.axis_size("dom")
    pairs = [(i, i + step) for i in range(count) if 0 <= i + step < count]
    return lax.ppermute(value, "dom", pairs)


def others(value, groups):
    size = len(groups[0])
    return [
        lax.ppermute(value, "dom", [(g[i], g[(i + s) % size]) for g in groups for i in range(size)])
        for s in range(1, size)
    ]


def whole(shape):
    return pl.BlockSpec(shape, lambda t: (0,) * len(shape))


def on_device(
    mode_shapes,
    eigenvalues,
    mode_weights,
    stiff_deriv,
    mass_ref,
    mass_scale,
    connectivity,
    design_owner,
    direction,
):
    modes, _, nodes = mode_shapes.shape
    elems = connectivity.shape[1]
    des = direction.shape[0]
    groups = lax.axis_size("mode")
    total_modes = groups * modes
    rows = COMPS * modes
    big = CORNERS * rows
    tiles = elems // TILE
    entries = 16

    dir_own = direction.reshape(1, des)
    dir_low, dir_high = neighbour(dir_own, 1), neighbour(dir_own, -1)
    field = jnp.transpose(mode_shapes, (1, 0, 2)).reshape(rows, nodes)
    rim = jnp.concatenate(
        [neighbour(field[:, nodes - H :], 1), neighbour(field[:, :H], -1)], axis=1
    )
    fields = [field] + [shift_in(field, "mode", s) for s in range(1, groups)]
    rims = [rim] + [shift_in(rim, "mode", s) for s in range(1, groups)]
    eig_row = eigenvalues.reshape(1, total_modes)
    weight_row = mode_weights.reshape(1, modes)
    mass_row = mass_scale.reshape(1, elems)
    owner_row = design_owner.reshape(1, elems)

    def tiled(rows_):
        return pl.BlockSpec((rows_, TILE), lambda t: (0, t))

    resid, power, node, node_rim, diag = pl.pallas_call(
        functools.partial(forces_kernel, modes, nodes, des),
        grid=(tiles,),
        in_specs=[
            tiled(CORNERS),
            tiled(1),
            tiled(1),
            pl.BlockSpec((DOFS, DOFS, TILE), lambda t: (0, 0, t)),
            whole((rows, nodes)),
            whole((rows, 2 * H)),
            whole((1, des)),
            whole((1, des)),
            whole((1, des)),
            whole((DOFS, DOFS)),
            whole((1, total_modes)),
            whole((1, modes)),
        ],
        out_specs=[
            tiled(big),
            tiled(modes),
            whole((rows, nodes)),
            whole((rows, 2 * H)),
            whole((modes, LANES)),
        ],
        out_shape=[
            jax.ShapeDtypeStruct((big, elems), f32),
            jax.ShapeDtypeStruct((modes, elems), f32),
            jax.ShapeDtypeStruct((rows, nodes), f32),
            jax.ShapeDtypeStruct((rows, 2 * H), f32),
            jax.ShapeDtypeStruct((modes, LANES), f32),
        ],
        scratch_shapes=[
            pltpu.VMEM((big, big), bf16),
            pltpu.VMEM((entries, LANES), f32),
            pltpu.VMEM((nodes, CORNERS * TILE), bf16),
            pltpu.VMEM((2 * H, CORNERS * TILE), bf16),
            pltpu.VMEM((rows, CORNERS * TILE), f32),
            pltpu.VMEM((big, TILE), bf16),
            pltpu.VMEM((big, TILE), f32),
            pltpu.VMEM((DOFS, DOFS, TILE), f32),
            pltpu.VMEM((rows, CORNERS * TILE), bf16),
        ],
        compiler_params=pltpu.CompilerParams(vmem_limit_bytes=40 * MIB),
        cost_estimate=pl.CostEstimate(
            flops=8_000_000_000, bytes_accessed=8_000_000, transcendentals=0
        ),
        name="forces",
    )(
        connectivity,
        owner_row,
        mass_row,
        stiff_deriv,
        field,
        rim,
        dir_low,
        dir_own,
        dir_high,
        mass_ref,
        eig_row,
        weight_row,
    )

    gram = pl.pallas_call(
        functools.partial(gram_kernel, modes, groups),
        out_shape=jax.ShapeDtypeStruct((modes + 8, total_modes), f32),
        compiler_params=pltpu.CompilerParams(vmem_limit_bytes=40 * MIB),
        name="gram",
    )(node, node_rim, diag, *fields, *rims)

    count = lax.axis_size("dom")
    cores = [[i, i + 1] for i in range(0, count, 2)]
    along_x = [[y * 8 + x * 2 + c for x in range(4)] for y in range(count // 8) for c in range(2)]
    along_y = [[y * 8 + k for y in range(count // 8)] for k in range(8)]
    for part in (cores, along_x):
        gram = sum(others(gram, part), gram)
    grams = [gram] + others(gram, along_y)

    low, own, high, eig_deriv = pl.pallas_call(
        functools.partial(energy_kernel, modes, groups, nodes, des, len(grams)),
        grid=(tiles,),
        in_specs=[whole(gram.shape)] * len(grams)
        + [whole((1, total_modes)), whole((1, modes))]
        + [whole((rows, nodes))] * groups
        + [whole((rows, 2 * H))] * groups
        + [tiled(CORNERS), tiled(1), tiled(big), tiled(modes)],
        out_specs=[whole((1, des))] * 3 + [whole((1, modes))],
        out_shape=[jax.ShapeDtypeStruct((1, des), f32)] * 3 + [jax.ShapeDtypeStruct((1, modes), f32)],
        scratch_shapes=[
            pltpu.VMEM((rows, nodes), bf16),
            pltpu.VMEM((rows, 2 * H), bf16),
            pltpu.VMEM((modes, LANES), f32),
            pltpu.VMEM((nodes, CORNERS * TILE), bf16),
            pltpu.VMEM((2 * H, CORNERS * TILE), bf16),
            pltpu.VMEM((entries, LANES), f32),
        ],
        compiler_params=pltpu.CompilerParams(vmem_limit_bytes=40 * MIB),
        name="energy",
    )(*grams, eig_row, weight_row, *fields, *rims, connectivity, owner_row, resid, power)

    owned = own + neighbour(low, -1) + neighbour(high, 1)
    for_all = owned
    for s in range(1, groups):
        for_all = for_all + shift_in(owned, "mode", s)
    return (for_all.reshape(des), eig_deriv.reshape(modes))


def solution(mesh):
    return jax.shard_map(
        on_device,
        mesh=mesh,
        in_specs=(
            P("mode", None, "dom"),
            P(),
            P("mode"),
            P(None, None, "dom"),
            P(),
            P("dom"),
            P(None, "dom"),
            P("dom"),
            P("dom"),
        ),
        out_specs=(P("dom"), P("mode")),
        check_vma=False,
    )
```

```python
import functools

import jax
import jax.numpy as jnp
from jax import lax
from jax.experimental import pallas as pl
from jax.experimental.pallas import tpu as pltpu
from jax.sharding import PartitionSpec as P

H = 32
COMPS = 6
CORNERS = 4
DOFS = 24
TILE = 256
LANES = 128
EXTRA = 16
MIB = 1 << 20
f32, bf16 = jnp.float32, jnp.bfloat16


def dot(a, b):
    return lax.dot_general(a, b, (((1,), (0,)), ((), ())), preferred_element_type=f32)


def dot_nt(a, b):
    return lax.dot_general(a, b, (((1,), (1,)), ((), ())), preferred_element_type=f32)


def iota(shape, dim):
    return lax.broadcasted_iota(jnp.int32, shape, dim)


def one_hot(rows, index):
    hit = iota((rows, index.shape[1]), 0) == index
    return jnp.where(hit, 1.0, 0.0).astype(bf16)


def three_pieces(x):
    first = x.astype(bf16)
    rest = x - first.astype(f32)
    second = rest.astype(bf16)
    third = (rest - second.astype(f32)).astype(bf16)
    return first, second, third


def column_of(row, offset, count):
    n = row.shape[1]
    mask = iota((count, n), 1) == iota((count, n), 0) + offset
    return jnp.sum(jnp.where(mask, row, 0.0), axis=1, keepdims=True)


def rim_one_hot(conn_ref, rim_hot, nodes):
    for k in range(CORNERS):
        index = conn_ref[k : k + 1, :]
        rim = jnp.where(
            index < H, index + (LANES - H), jnp.where(index < nodes + H, -1, index - (nodes + H))
        )
        rim_hot[:, k * TILE : (k + 1) * TILE] = one_hot(LANES, rim)


def pack_kernel(rows, des, first_ref, last_ref, dir_ref, owner_ref, mass_ref_, up_ref, down_ref, owner_row, mass_row):
    up_ref[0:rows, :] = last_ref[...]
    down_ref[0:rows, :] = first_ref[...]
    table = jnp.concatenate(
        [dir_ref[i * LANES : (i + 1) * LANES].reshape(1, LANES) for i in range(des // LANES)], axis=0
    )
    pieces = [p.astype(f32) for p in three_pieces(table)]
    pad = jnp.zeros((EXTRA - 3 * (des // LANES), LANES), f32)
    packed = jnp.concatenate(pieces + [pad], axis=0).astype(bf16)
    up_ref[rows : rows + EXTRA, :] = packed
    down_ref[rows : rows + EXTRA, :] = packed
    for i in range(owner_row.shape[1] // LANES):
        span = slice(i * LANES, (i + 1) * LANES)
        owner_row[:, span] = owner_ref[span].reshape(1, LANES)
        mass_row[:, span] = mass_ref_[span].reshape(1, LANES)


def prepare_kernel(modes, nodes, conn_ref, field_ref, ref_ref, own_hot, shapes, mass_big):
    rows = COMPS * modes
    big = CORNERS * rows

    @pl.when(pl.program_id(0) == 0)
    def _():
        row = iota((big, DOFS), 0)
        dof = CORNERS * ((row % rows) // modes) + row // rows
        spread = jnp.where(dof == iota((big, DOFS), 1), 1.0, 0.0).astype(bf16)
        half = dot(spread, ref_ref[...]).astype(bf16)
        same = iota((big, rows), 0) % modes == iota((big, rows), 1) % modes
        for part in range(CORNERS):
            wide = dot_nt(half, spread[part * rows : (part + 1) * rows])
            mass_big[:, part * rows : (part + 1) * rows] = jnp.where(same, wide, 0.0).astype(bf16)

    for k in range(CORNERS):
        own_hot[:, k * TILE : (k + 1) * TILE] = one_hot(nodes, conn_ref[k : k + 1, :] - H)
    shapes[...] = dot(field_ref[...], own_hot[...]).astype(bf16)


def forces_kernel(
    modes,
    nodes,
    des,
    conn_ref,
    owner_ref,
    mass_ref_,
    stiff_ref,
    own_hot,
    own_shapes,
    low_ref,
    own_ref,
    high_ref,
    mass_big,
    eig_ref,
    weight_ref,
    resid_ref,
    power_ref,
    node_ref,
    node_rim_ref,
    diag_ref,
    table,
    rim,
    rim_hot,
    shapes,
    stacked,
    mass_q,
    stiff_wide,
    force,
):
    step = pl.program_id(0)
    rows = COMPS * modes
    rank = lax.axis_index("dom")
    mode_start = lax.axis_index("mode") * modes
    entries = table.shape[0] // 3

    @pl.when(step == 0)
    def _():
        per = des // LANES
        sides = []
        for ref in (low_ref, own_ref, high_ref):
            packed = ref[rows : rows + EXTRA, :].astype(f32)
            sides.append(packed[:per] + packed[per : 2 * per] + packed[2 * per : 3 * per])
        sides.append(jnp.zeros((entries - 3 * per, LANES), f32))
        for i, piece in enumerate(three_pieces(jnp.concatenate(sides, axis=0))):
            table[i * entries : (i + 1) * entries, :] = piece
        lower = iota((rows, LANES), 1) >= LANES // 2
        rim[...] = jnp.where(lower, low_ref[0:rows, :].astype(f32), high_ref[0:rows, :].astype(f32)).astype(bf16)
        node_ref[...] = jnp.zeros_like(node_ref)
        node_rim_ref[...] = jnp.zeros_like(node_rim_ref)
        diag_ref[...] = jnp.zeros_like(diag_ref)

    eig = column_of(eig_ref[...], mode_start, modes)
    weight = 2.0 * column_of(weight_ref[...], 0, modes)

    local = owner_ref[...] - (rank - 1) * des
    looked = dot(table[...], one_hot(LANES, local % LANES))
    looked = looked[:entries] + looked[entries : 2 * entries] + looked[2 * entries :]
    here = iota((entries, TILE), 0) == local // LANES
    elem_dir = jnp.sum(jnp.where(here, looked, 0.0), axis=0, keepdims=True)
    elem_mass = mass_ref_[...]

    rim_one_hot(conn_ref, rim_hot, nodes)
    shapes[...] = own_shapes[...].astype(f32) + dot(rim[...], rim_hot[...])
    for k in range(CORNERS):
        stacked[k * rows : (k + 1) * rows, :] = shapes[:, k * TILE : (k + 1) * TILE].astype(bf16)
    mass_q[...] = dot(mass_big[...], stacked[...])
    stiff_wide[...] = stiff_ref[...].astype(f32)

    for lane in range(TILE // LANES):
        cols = slice(lane * LANES, (lane + 1) * LANES)
        direction = elem_dir[:, cols]
        mass = elem_mass[:, cols]
        scaled = eig * mass
        power = jnp.zeros((modes, LANES), f32)
        for first in range(0, DOFS, 4):
            sums = [jnp.zeros((modes, LANES), f32) for _ in range(4)]
            for b in range(DOFS):
                c, k = b // CORNERS, b % CORNERS
                at = k * TILE + lane * LANES
                s = shapes[c * modes : (c + 1) * modes, at : at + LANES]
                for q in range(4):
                    sums[q] = sums[q] + stiff_wide[first + q, b : b + 1, cols] * s
            for q in range(4):
                c, k = (first + q) // CORNERS, (first + q) % CORNERS
                at = k * TILE + lane * LANES
                s = shapes[c * modes : (c + 1) * modes, at : at + LANES]
                base = k * rows + c * modes
                mq = mass_q[base : base + modes, cols]
                power = power + s * mq
                resid = sums[q] - scaled * mq
                force[c * modes : (c + 1) * modes, at : at + LANES] = (direction * resid).astype(bf16)
                resid_ref[base : base + modes, cols] = weight * resid
        power = power * mass
        power_ref[:, cols] = power
        diag_ref[...] += direction * power

    node_ref[...] += dot_nt(force[...], own_hot[...])
    node_rim_ref[...] += dot_nt(force[...], rim_hot[...])


def gather_modes(ref, c, modes, groups):
    rows = COMPS * modes
    return jnp.concatenate(
        [ref[g * rows + c * modes : g * rows + (c + 1) * modes, :] for g in range(groups)], axis=0
    )


def gram_kernel(modes, groups, node_ref, node_rim_ref, diag_ref, fields, rims, out_ref):
    mode_start = lax.axis_index("mode") * modes
    total = jnp.zeros((modes, groups * modes), f32)
    for c in range(COMPS):
        span = slice(c * modes, (c + 1) * modes)
        for part, parts in ((node_ref, fields), (node_rim_ref, rims)):
            exact = part[span, :]
            high = exact.astype(bf16)
            low = (exact - high.astype(f32)).astype(bf16)
            both = dot_nt(
                jnp.concatenate([high, low], axis=0), gather_modes(parts, c, modes, groups)
            )
            total = total + both[:modes] + both[modes:]
    out_ref[0:modes, :] = total
    diag = jnp.sum(diag_ref[...], axis=1, keepdims=True)
    mask = iota((modes, LANES), 0) == iota((modes, LANES), 1)
    out_ref[modes : modes + 8, :] = jnp.broadcast_to(
        jnp.sum(jnp.where(mask, diag, 0.0), axis=0, keepdims=True), (8, LANES)
    )


def energy_kernel(
    modes,
    groups,
    nodes,
    des,
    gram_ref,
    eig_ref,
    weight_ref,
    fields,
    rims,
    conn_ref,
    owner_ref,
    own_hot,
    resid_ref,
    power_ref,
    low_ref,
    own_ref,
    high_ref,
    deriv_ref,
    deriv,
    deriv_rim,
    factor,
    rim_hot,
    totals,
):
    step = pl.program_id(0)
    rows = COMPS * modes
    rank = lax.axis_index("dom")
    mode_start = lax.axis_index("mode") * modes

    @pl.when(step == 0)
    def _():
        total = gram_ref[0]
        for i in range(1, gram_ref.shape[0]):
            total = total + gram_ref[i]
        gram = total[:modes]
        mass_diag = column_of(total[modes : modes + 1], 0, modes)
        shape = (modes, groups * modes)
        mask = iota(shape, 0) + mode_start == iota(shape, 1)
        eig_row = eig_ref[...]
        spacing = column_of(eig_row, mode_start, modes) - eig_row
        combiner = jnp.where(
            mask, -0.5 * mass_diag, gram / jnp.where(mask, 1.0, spacing)
        ).astype(bf16)
        eig_deriv = jnp.sum(jnp.where(mask, gram, 0.0), axis=1, keepdims=True)
        small = iota((modes, modes), 0) == iota((modes, modes), 1)
        deriv_ref[...] = jnp.sum(jnp.where(small, eig_deriv, 0.0), axis=0, keepdims=True)
        factor[...] = jnp.broadcast_to(
            eig_deriv * column_of(weight_ref[...], 0, modes), factor.shape
        )
        for c in range(COMPS):
            span = slice(c * modes, (c + 1) * modes)
            deriv[span, :] = dot(combiner, gather_modes(fields, c, modes, groups)).astype(bf16)
            deriv_rim[span, :] = dot(combiner, gather_modes(rims, c, modes, groups)).astype(bf16)
        totals[...] = jnp.zeros_like(totals)

    rim_one_hot(conn_ref, rim_hot, nodes)
    moved = dot(deriv[...], own_hot[...]) + dot(deriv_rim[...], rim_hot[...])
    energies = []
    for lane in range(TILE // LANES):
        cols = slice(lane * LANES, (lane + 1) * LANES)
        total = -factor[...] * power_ref[:, cols]
        for k in range(CORNERS):
            at = k * TILE + lane * LANES
            for c in range(COMPS):
                base = k * rows + c * modes
                total = total + moved[c * modes : (c + 1) * modes, at : at + LANES] * resid_ref[
                    base : base + modes, cols
                ]
        energies.append(jnp.sum(total, axis=0, keepdims=True))
    energy = jnp.concatenate(energies, axis=1)
    local = owner_ref[...] - (rank - 1) * des
    entries = totals.shape[0]
    here = iota((entries, TILE), 0) == local // LANES
    spread = jnp.concatenate(
        [jnp.where(here, p.astype(f32), 0.0).astype(bf16) for p in three_pieces(energy)], axis=0
    )
    sums = dot_nt(spread, one_hot(LANES, local % LANES))
    totals[...] += sums[:entries] + sums[entries : 2 * entries] + sums[2 * entries :]

    @pl.when(step == pl.num_programs(0) - 1)
    def _():
        per = des // LANES
        for side, ref in enumerate((low_ref, own_ref, high_ref)):
            for i in range(per):
                at = side * per + i
                ref[:, i * LANES : (i + 1) * LANES] = totals[at : at + 1, :]


def neighbour(value, step):
    count = lax.axis_size("dom")
    pairs = [(i, i + step) for i in range(count) if 0 <= i + step < count]
    return lax.ppermute(value, "dom", pairs)


def from_all(value, axis, groups):
    size = len(groups[0])
    copies = jnp.broadcast_to(value[None], (size,) + value.shape)
    return lax.all_to_all(copies, axis, 0, 0, axis_index_groups=groups)


def whole(shape):
    return pl.BlockSpec(shape, lambda t: (0,) * len(shape))


def tiled(rows):
    return pl.BlockSpec((rows, TILE), lambda t: (0, t))


def params(mib):
    return pltpu.CompilerParams(vmem_limit_bytes=mib * MIB)


def cost(flops, bytes_):
    return pl.CostEstimate(flops=flops, bytes_accessed=bytes_, transcendentals=0)


def on_device(
    mode_shapes,
    eigenvalues,
    mode_weights,
    stiff_deriv,
    mass_ref,
    mass_scale,
    connectivity,
    design_owner,
    direction,
):
    modes, _, nodes = mode_shapes.shape
    elems = connectivity.shape[1]
    des = direction.shape[0]
    groups = lax.axis_size("mode")
    count = lax.axis_size("dom")
    total_modes = groups * modes
    rows = COMPS * modes
    big = CORNERS * rows
    tiles = elems // TILE
    wide = CORNERS * TILE
    entries = 16
    shaped = jax.ShapeDtypeStruct
    wide_tile = pl.BlockSpec((nodes, wide), lambda t: (0, t))
    shape_tile = pl.BlockSpec((rows, wide), lambda t: (0, t))

    field = jnp.transpose(mode_shapes, (1, 0, 2)).reshape(rows, nodes)
    fields = lax.all_gather(field, "mode", axis=0, tiled=True)
    eig_row = eigenvalues.reshape(1, total_modes)
    weight_row = mode_weights.reshape(1, modes)

    up, down, owner_row, mass_row = pl.pallas_call(
        functools.partial(pack_kernel, rows, des),
        grid=(1,),
        in_specs=[
            pl.BlockSpec((rows, LANES), lambda t: (0, 0)),
            pl.BlockSpec((rows, LANES), lambda t: (0, nodes // LANES - 1)),
            whole((des,)),
            whole((elems,)),
            whole((elems,)),
        ],
        out_specs=[whole((rows + EXTRA, LANES))] * 2 + [whole((1, elems))] * 2,
        out_shape=[shaped((rows + EXTRA, LANES), bf16)] * 2
        + [shaped((1, elems), jnp.int32), shaped((1, elems), f32)],
        name="pack",
    )(field, field, direction, design_owner, mass_scale)
    low, high = neighbour(up, 1), neighbour(down, -1)

    own_hot, own_shapes, mass_big = pl.pallas_call(
        functools.partial(prepare_kernel, modes, nodes),
        grid=(tiles,),
        in_specs=[tiled(CORNERS), whole((rows, nodes)), whole((DOFS, DOFS))],
        out_specs=[wide_tile, shape_tile, whole((big, big))],
        out_shape=[
            shaped((nodes, CORNERS * elems), bf16),
            shaped((rows, CORNERS * elems), bf16),
            shaped((big, big), bf16),
        ],
        compiler_params=params(24),
        cost_estimate=cost(4_000_000_000, 8_000_000),
        name="prepare",
    )(connectivity, field, mass_ref)

    upper = lax.broadcasted_iota(jnp.int32, (rows, LANES), 1) < LANES // 2
    rims = lax.all_gather(jnp.where(upper, high[:rows], low[:rows]), "mode", axis=0, tiled=True)

    resid, power, node, node_rim, diag = pl.pallas_call(
        functools.partial(forces_kernel, modes, nodes, des),
        grid=(tiles,),
        in_specs=[
            tiled(CORNERS),
            tiled(1),
            tiled(1),
            pl.BlockSpec((DOFS, DOFS, TILE), lambda t: (0, 0, t)),
            wide_tile,
            shape_tile,
            whole((rows + EXTRA, LANES)),
            whole((rows + EXTRA, LANES)),
            whole((rows + EXTRA, LANES)),
            whole((big, big)),
            whole((1, total_modes)),
            whole((1, modes)),
        ],
        out_specs=[
            tiled(big),
            tiled(modes),
            whole((rows, nodes)),
            whole((rows, LANES)),
            whole((modes, LANES)),
        ],
        out_shape=[
            shaped((big, elems), f32),
            shaped((modes, elems), f32),
            shaped((rows, nodes), f32),
            shaped((rows, LANES), f32),
            shaped((modes, LANES), f32),
        ],
        scratch_shapes=[
            pltpu.VMEM((3 * entries, LANES), bf16),
            pltpu.VMEM((rows, LANES), bf16),
            pltpu.VMEM((LANES, wide), bf16),
            pltpu.VMEM((rows, wide), f32),
            pltpu.VMEM((big, TILE), bf16),
            pltpu.VMEM((big, TILE), f32),
            pltpu.VMEM((DOFS, DOFS, TILE), f32),
            pltpu.VMEM((rows, wide), bf16),
        ],
        compiler_params=params(24),
        cost_estimate=cost(8_000_000_000, 8_000_000),
        name="forces",
    )(
        connectivity,
        owner_row,
        mass_row,
        stiff_deriv,
        own_hot,
        own_shapes,
        low,
        up,
        high,
        mass_big,
        eig_row,
        weight_row,
    )

    gram = pl.pallas_call(
        functools.partial(gram_kernel, modes, groups),
        out_shape=shaped((modes + 8, total_modes), f32),
        compiler_params=params(24),
        name="gram",
    )(node, node_rim, diag, fields, rims)

    gram = gram + lax.ppermute(gram, "dom", [(i, i ^ 1) for i in range(count)])
    grams = from_all(gram, "dom", [list(range(core, count, 2)) for core in range(2)])

    low_sum, own_sum, high_sum, eig_deriv = pl.pallas_call(
        functools.partial(energy_kernel, modes, groups, nodes, des),
        grid=(tiles,),
        in_specs=[
            whole(grams.shape),
            whole((1, total_modes)),
            whole((1, modes)),
            whole((groups * rows, nodes)),
            whole((groups * rows, LANES)),
            tiled(CORNERS),
            tiled(1),
            wide_tile,
            tiled(big),
            tiled(modes),
        ],
        out_specs=[whole((1, des))] * 3 + [whole((1, modes))],
        out_shape=[shaped((1, des), f32)] * 3 + [shaped((1, modes), f32)],
        scratch_shapes=[
            pltpu.VMEM((rows, nodes), bf16),
            pltpu.VMEM((rows, LANES), bf16),
            pltpu.VMEM((modes, LANES), f32),
            pltpu.VMEM((LANES, wide), bf16),
            pltpu.VMEM((entries, LANES), f32),
        ],
        compiler_params=params(24),
        name="energy",
    )(grams, eig_row, weight_row, fields, rims, connectivity, owner_row, own_hot, resid, power)

    owned = own_sum + neighbour(low_sum, -1) + neighbour(high_sum, 1)
    hess_vec = jnp.sum(from_all(owned, "mode", [list(range(groups))]), axis=0)
    return (hess_vec.reshape(des), eig_deriv.reshape(modes))


def solution(mesh):
    return jax.shard_map(
        on_device,
        mesh=mesh,
        in_specs=(
            P("mode", None, "dom"),
            P(),
            P("mode"),
            P(None, None, "dom"),
            P(),
            P("dom"),
            P(None, "dom"),
            P("dom"),
            P("dom"),
        ),
        out_specs=(P("dom"), P("mode")),
        check_vma=False,
    )
```

```python
import functools

import jax
import jax.numpy as jnp
from jax import lax
from jax.experimental import pallas as pl
from jax.experimental.pallas import tpu as pltpu
from jax.sharding import PartitionSpec as P

H = 32
COMPS = 6
CORNERS = 4
DOFS = 24
TILE = 256
LANES = 128
EXTRA = 16
SUBS = 8
MIB = 1 << 20
f32, bf16 = jnp.float32, jnp.bfloat16


def dot(a, b):
    return lax.dot_general(a, b, (((1,), (0,)), ((), ())), preferred_element_type=f32)


def dot_nt(a, b):
    return lax.dot_general(a, b, (((1,), (1,)), ((), ())), preferred_element_type=f32)


def iota(shape, dim):
    return lax.broadcasted_iota(jnp.int32, shape, dim)


def one_hot(rows, index):
    hit = iota((rows, index.shape[1]), 0) == index
    return jnp.where(hit, 1.0, 0.0).astype(bf16)


def three_pieces(x):
    first = x.astype(bf16)
    rest = x - first.astype(f32)
    second = rest.astype(bf16)
    third = (rest - second.astype(f32)).astype(bf16)
    return first, second, third


def column_of(row, offset, count):
    n = row.shape[1]
    mask = iota((count, n), 1) == iota((count, n), 0) + offset
    return jnp.sum(jnp.where(mask, row, 0.0), axis=1, keepdims=True)


def pack_kernel(rows, des, first_ref, last_ref, dir_ref, up_ref, down_ref):
    up_ref[0:rows, :] = last_ref[...]
    down_ref[0:rows, :] = first_ref[...]
    table = jnp.concatenate(
        [dir_ref[i * LANES : (i + 1) * LANES].reshape(1, LANES) for i in range(des // LANES)], axis=0
    )
    pieces = [p.astype(f32) for p in three_pieces(table)]
    pad = jnp.zeros((EXTRA - 3 * (des // LANES), LANES), f32)
    packed = jnp.concatenate(pieces + [pad], axis=0).astype(bf16)
    up_ref[rows : rows + EXTRA, :] = packed
    down_ref[rows : rows + EXTRA, :] = packed


def fill_one_hot(conn_ref, at, hot, nodes):
    for k in range(CORNERS):
        index = conn_ref[k : k + 1, pl.ds(at, TILE)]
        index = jnp.where(index < H, index + (nodes + LANES - H), index - H)
        hot[:, k * TILE : (k + 1) * TILE] = one_hot(nodes + LANES, index)


def rows_of(flat_ref, row_ref):
    for i in range(row_ref.shape[1] // LANES):
        span = slice(i * LANES, (i + 1) * LANES)
        row_ref[:, span] = flat_ref[span].reshape(1, LANES)


def expand_mass(ref):
    size = DOFS * SUBS
    spread = jnp.where(iota((size, DOFS), 0) // SUBS == iota((size, DOFS), 1), 1.0, 0.0).astype(bf16)
    full = dot_nt(dot(spread, ref).astype(bf16), spread)
    same = iota((size, size), 0) % SUBS == iota((size, size), 1) % SUBS
    return jnp.where(same, full, 0.0).astype(bf16)


def forces_kernel(
    modes,
    nodes,
    des,
    elems,
    conn_hbm,
    owner_hbm,
    mass_hbm,
    stiff_hbm,
    field_hbm,
    ref_hbm,
    eig_hbm,
    weight_hbm,
    low_ref,
    own_ref,
    high_ref,
    resid_ref,
    power_ref,
    node_ref,
    conn,
    owner_row,
    eig_row,
    weight_row,
    owner_flat,
    mass_flat,
    stiff,
    field,
    ref,
    sems,
    stiff_sems,
    mass_row,
    dir_row,
    mass_big,
    hot,
    shapes,
    mass_q,
    stiff_wide,
    force,
    sums_t,
):
    rows = COMPS * modes
    tiles = elems // TILE
    rank = lax.axis_index("dom")
    mode_start = lax.axis_index("mode") * modes
    entries = 16
    small = [
        pltpu.make_async_copy(source, target, sems.at[i])
        for i, (source, target) in enumerate(
            (
                (ref_hbm, ref),
                (conn_hbm, conn),
                (field_hbm, field.at[:, pl.ds(0, nodes)]),
                (owner_hbm, owner_flat),
                (mass_hbm, mass_flat),
                (eig_hbm, eig_row),
                (weight_hbm, weight_row),
            )
        )
    ]

    def stiff_copy(t):
        cols = pl.ds(pl.multiple_of(t * TILE, TILE), TILE)
        return pltpu.make_async_copy(stiff_hbm.at[:, :, cols], stiff.at[t], stiff_sems.at[t])

    for copy in small:
        copy.start()
    for t in range(tiles):
        stiff_copy(t).start()

    per = des // LANES
    sides = []
    for ref_ in (low_ref, own_ref, high_ref):
        packed = ref_[rows : rows + EXTRA, :].astype(f32)
        sides.append(packed[:per] + packed[per : 2 * per] + packed[2 * per : 3 * per])
    sides.append(jnp.zeros((entries - 3 * per, LANES), f32))
    table = jnp.concatenate(three_pieces(jnp.concatenate(sides, axis=0)), axis=0)
    lower = iota((rows, LANES), 1) >= LANES // 2
    field[:, nodes : nodes + LANES] = jnp.where(
        lower, low_ref[0:rows, :].astype(f32), high_ref[0:rows, :].astype(f32)
    ).astype(bf16)
    sums_t[...] = jnp.zeros_like(sums_t)
    for copy in small:
        copy.wait()
    mass_big[...] = expand_mass(ref[...])
    rows_of(owner_flat, owner_row)
    rows_of(mass_flat, mass_row)
    eig = column_of(eig_row[...], mode_start, modes)
    weight = 2.0 * column_of(weight_row[...], 0, modes)
    local = owner_row[...] - (rank - 1) * des
    looked = dot(table, one_hot(LANES, local % LANES))
    looked = looked[:entries] + looked[entries : 2 * entries] + looked[2 * entries :]
    here = iota((entries, elems), 0) == local // LANES
    dir_row[...] = jnp.sum(jnp.where(here, looked, 0.0), axis=0, keepdims=True)

    @pl.loop(0, tiles)
    def _(t):
        at = pl.multiple_of(t * TILE, TILE)
        elem_dir = dir_row[:, pl.ds(at, TILE)]
        elem_mass = mass_row[:, pl.ds(at, TILE)]
        fill_one_hot(conn, at, hot, nodes)
        shapes[...] = dot(field[...], hot[...])
        for g in range(modes // SUBS):
            stacked = [
                shapes[
                    (b // CORNERS) * modes + g * SUBS : (b // CORNERS) * modes + (g + 1) * SUBS,
                    (b % CORNERS) * TILE : (b % CORNERS + 1) * TILE,
                ]
                for b in range(DOFS)
            ]
            mass_q[g] = dot(mass_big[...], jnp.concatenate(stacked, axis=0).astype(bf16))
        stiff_copy(t).wait()
        stiff_wide[...] = stiff[t].astype(f32)

        for lane in range(TILE // LANES):
            cols = slice(lane * LANES, (lane + 1) * LANES)
            at_lane = pl.multiple_of(at + lane * LANES, LANES)
            direction = elem_dir[:, cols]
            mass = elem_mass[:, cols]
            scaled = eig * mass
            dir_mass = direction * mass
            power = jnp.zeros((modes, LANES), f32)
            for first in range(0, DOFS, 4):
                sums = [jnp.zeros((modes, LANES), f32) for _ in range(4)]
                for b in range(DOFS):
                    c, k = b // CORNERS, b % CORNERS
                    col = k * TILE + lane * LANES
                    s = shapes[c * modes : (c + 1) * modes, col : col + LANES]
                    for q in range(4):
                        sums[q] = sums[q] + stiff_wide[first + q, b : b + 1, cols] * s
                for q in range(4):
                    c, k = (first + q) // CORNERS, (first + q) % CORNERS
                    col = k * TILE + lane * LANES
                    s = shapes[c * modes : (c + 1) * modes, col : col + LANES]
                    base = k * rows + c * modes
                    mq = jnp.concatenate(
                        [
                            mass_q[g, (first + q) * SUBS : (first + q + 1) * SUBS, cols]
                            for g in range(modes // SUBS)
                        ],
                        axis=0,
                    )
                    power = power + s * mq
                    span = slice(c * modes, (c + 1) * modes)
                    force[span, col : col + LANES] = (direction * sums[q]).astype(bf16)
                    span = slice(rows + c * modes, rows + (c + 1) * modes)
                    force[span, col : col + LANES] = (dir_mass * mq).astype(bf16)
                    resid_ref[base : base + modes, pl.ds(at_lane, LANES)] = weight * (
                        sums[q] - scaled * mq
                    )
            power_ref[:, pl.ds(at_lane, LANES)] = power * mass

        sums_t[...] += dot_nt(hot[...], force[...])

    for i in range((nodes + LANES) // LANES):
        span = slice(i * LANES, (i + 1) * LANES)
        for part in range(2 * rows // LANES):
            node_ref[part * LANES : (part + 1) * LANES, span] = sums_t[
                span, part * LANES : (part + 1) * LANES
            ].T


def gather_modes(refs, c, modes):
    return jnp.concatenate([r[c * modes : (c + 1) * modes, :] for r in refs], axis=0)


def gram_kernel(modes, groups, nodes, node_ref, eig_ref, *refs):
    fields, rims, out_ref = refs[:groups], refs[groups : 2 * groups], refs[2 * groups]
    rows = COMPS * modes
    eig = column_of(eig_ref[...], lax.axis_index("mode") * modes, modes)
    grams = [jnp.zeros((modes, groups * modes), f32) for _ in range(2)]
    for c in range(COMPS):
        for cols, parts in ((slice(0, nodes), fields), (slice(nodes, nodes + LANES), rims)):
            pieces = []
            for kind in range(2):
                base = kind * rows + c * modes
                pieces += three_pieces(node_ref[base : base + modes, cols])
            each = dot_nt(jnp.concatenate(pieces, axis=0), gather_modes(parts, c, modes))
            each = [each[i * modes : (i + 1) * modes] for i in range(6)]
            grams = [grams[k] + (each[3 * k] + (each[3 * k + 1] + each[3 * k + 2])) for k in range(2)]
    stiff_gram, mass_gram = grams
    out_ref[0:modes, :] = stiff_gram - eig * mass_gram
    mask = iota(mass_gram.shape, 0) == iota(mass_gram.shape, 1)
    out_ref[modes : modes + 8, :] = jnp.broadcast_to(
        jnp.sum(jnp.where(mask, mass_gram, 0.0), axis=0, keepdims=True), (8, LANES)
    )


def energy_kernel(modes, groups, nodes, des, elems, gram_ref, eig_ref, weight_ref, *refs):
    fields, rims, refs = refs[:groups], refs[groups : 2 * groups], refs[2 * groups :]
    conn_ref, owner_row, resid_ref, power_ref = refs[:4]
    low_ref, own_ref, high_ref, deriv_ref = refs[4:8]
    deriv, factor, hot, totals = refs[8:]
    rows = COMPS * modes
    rank = lax.axis_index("dom")
    mode_start = lax.axis_index("mode") * modes

    total = gram_ref[0]
    for i in range(1, gram_ref.shape[0]):
        total = total + gram_ref[i]
    gram = total[:modes]
    mass_diag = column_of(total[modes : modes + 1], 0, modes)
    shape = (modes, groups * modes)
    mask = iota(shape, 0) == iota(shape, 1)
    eig_rows = jnp.broadcast_to(eig_ref[...], (8, LANES))
    turned = pltpu.roll(eig_rows, lax.rem(LANES - mode_start, LANES), 1)[0:1]
    spacing = column_of(turned, 0, modes) - turned
    combiner = jnp.where(mask, -0.5 * mass_diag, gram / jnp.where(mask, 1.0, spacing)).astype(bf16)
    diagonal = jnp.where(mask, gram, 0.0)
    deriv_ref[...] = jnp.sum(diagonal, axis=0, keepdims=True)[:, :modes]
    eig_deriv = jnp.sum(diagonal, axis=1, keepdims=True)
    factor[...] = jnp.broadcast_to(eig_deriv * column_of(weight_ref[...], 0, modes), factor.shape)
    for c in range(COMPS):
        span = slice(c * modes, (c + 1) * modes)
        deriv[span, 0:nodes] = dot(combiner, gather_modes(fields, c, modes)).astype(bf16)
        deriv[span, nodes : nodes + LANES] = dot(combiner, gather_modes(rims, c, modes)).astype(bf16)
    totals[...] = jnp.zeros_like(totals)

    @pl.loop(0, elems // TILE)
    def _(t):
        at = pl.multiple_of(t * TILE, TILE)
        fill_one_hot(conn_ref, at, hot, nodes)
        moved = dot(deriv[...], hot[...])
        energies = []
        for lane in range(TILE // LANES):
            cols = pl.ds(pl.multiple_of(at + lane * LANES, LANES), LANES)
            total = -factor[...] * power_ref[:, cols]
            for k in range(CORNERS):
                col = k * TILE + lane * LANES
                for c in range(COMPS):
                    base = k * rows + c * modes
                    total = total + moved[
                        c * modes : (c + 1) * modes, col : col + LANES
                    ] * resid_ref[base : base + modes, cols]
            energies.append(jnp.sum(total, axis=0, keepdims=True))
        energy = jnp.concatenate(energies, axis=1)
        local = owner_row[:, pl.ds(at, TILE)] - (rank - 1) * des
        entries = totals.shape[0]
        here = iota((entries, TILE), 0) == local // LANES
        spread = jnp.concatenate(
            [jnp.where(here, p.astype(f32), 0.0).astype(bf16) for p in three_pieces(energy)], axis=0
        )
        sums = dot_nt(spread, one_hot(LANES, local % LANES))
        totals[...] += sums[:entries] + sums[entries : 2 * entries] + sums[2 * entries :]

    per = des // LANES
    for side, ref in enumerate((low_ref, own_ref, high_ref)):
        for i in range(per):
            at = side * per + i
            ref[:, i * LANES : (i + 1) * LANES] = totals[at : at + 1, :]


def neighbour(value, step):
    count = lax.axis_size("dom")
    pairs = [(i, i + step) for i in range(count) if 0 <= i + step < count]
    return lax.ppermute(value, "dom", pairs)


def shift_in(value, axis, step):
    count = lax.axis_size(axis)
    return lax.ppermute(value, axis, [(i, (i - step) % count) for i in range(count)])


def from_all(value, axis, groups):
    size = len(groups[0])
    copies = jnp.broadcast_to(value[None], (size,) + value.shape)
    return lax.all_to_all(copies, axis, 0, 0, axis_index_groups=groups)


def whole(shape):
    return pl.BlockSpec(shape, lambda t: (0,) * len(shape))


def params(mib):
    return pltpu.CompilerParams(vmem_limit_bytes=mib * MIB)


def cost(flops, bytes_):
    return pl.CostEstimate(flops=flops, bytes_accessed=bytes_, transcendentals=0)


def on_device(
    mode_shapes,
    eigenvalues,
    mode_weights,
    stiff_deriv,
    mass_ref,
    mass_scale,
    connectivity,
    design_owner,
    direction,
):
    modes, _, nodes = mode_shapes.shape
    elems = connectivity.shape[1]
    des = direction.shape[0]
    groups = lax.axis_size("mode")
    count = lax.axis_size("dom")
    total_modes = groups * modes
    rows = COMPS * modes
    big = CORNERS * rows
    tiles = elems // TILE
    wide = CORNERS * TILE
    entries = 16
    shaped = jax.ShapeDtypeStruct
    vmem = pl.BlockSpec(memory_space=pltpu.VMEM)
    hbm = pl.BlockSpec(memory_space=pltpu.HBM)

    field = jnp.transpose(mode_shapes, (1, 0, 2)).reshape(rows, nodes)
    eig_row = eigenvalues.reshape(1, total_modes)
    weight_row = mode_weights.reshape(1, modes)

    up, down = pl.pallas_call(
        functools.partial(pack_kernel, rows, des),
        grid=(1,),
        in_specs=[
            pl.BlockSpec((rows, LANES), lambda t: (0, 0)),
            pl.BlockSpec((rows, LANES), lambda t: (0, nodes // LANES - 1)),
            whole((des,)),
        ],
        out_specs=[whole((rows + EXTRA, LANES))] * 2,
        out_shape=[shaped((rows + EXTRA, LANES), bf16)] * 2,
        name="pack",
    )(field, field, direction)
    low, high = neighbour(up, 1), neighbour(down, -1)
    upper = lax.broadcasted_iota(jnp.int32, (rows, LANES), 1) < LANES // 2
    rim = jnp.where(upper, high[:rows], low[:rows])
    fields = [field] + [shift_in(field, "mode", s) for s in range(1, groups)]
    rims = [rim] + [shift_in(rim, "mode", s) for s in range(1, groups)]

    def pinned(*values):
        return [pltpu.with_memory_space_constraint(v, pltpu.HBM) for v in values]

    resid, power, node, conn, owner_row, eig_copy, weight_copy = pl.pallas_call(
        functools.partial(forces_kernel, modes, nodes, des, elems),
        in_specs=[hbm] * 8 + [vmem] * 3,
        out_specs=[vmem] * 7,
        out_shape=[
            shaped((big, elems), f32),
            shaped((modes, elems), f32),
            shaped((2 * rows, nodes + LANES), f32),
            shaped((CORNERS, elems), jnp.int32),
            shaped((1, elems), jnp.int32),
            shaped((1, total_modes), f32),
            shaped((1, modes), f32),
        ],
        scratch_shapes=[
            pltpu.VMEM((elems,), jnp.int32),
            pltpu.VMEM((elems,), f32),
            pltpu.VMEM((tiles, DOFS, DOFS, TILE), bf16),
            pltpu.VMEM((rows, nodes + LANES), bf16),
            pltpu.VMEM((DOFS, DOFS), bf16),
            pltpu.SemaphoreType.DMA((7,)),
            pltpu.SemaphoreType.DMA((tiles,)),
            pltpu.VMEM((1, elems), f32),
            pltpu.VMEM((1, elems), f32),
            pltpu.VMEM((DOFS * SUBS, DOFS * SUBS), bf16),
            pltpu.VMEM((nodes + LANES, wide), bf16),
            pltpu.VMEM((rows, wide), f32),
            pltpu.VMEM((modes // SUBS, DOFS * SUBS, TILE), f32),
            pltpu.VMEM((DOFS, DOFS, TILE), f32),
            pltpu.VMEM((2 * rows, wide), bf16),
            pltpu.VMEM((nodes + LANES, 2 * rows), f32),
        ],
        compiler_params=params(24),
        cost_estimate=cost(8_000_000_000, 8_000_000),
        name="forces",
    )(
        *pinned(
            connectivity,
            design_owner,
            mass_scale,
            stiff_deriv,
            field,
            mass_ref,
            eig_row,
            weight_row,
        ),
        low,
        up,
        high,
    )

    gram = pl.pallas_call(
        functools.partial(gram_kernel, modes, groups, nodes),
        out_shape=shaped((modes + 8, total_modes), f32),
        compiler_params=params(24),
        name="gram",
    )(node, eig_copy, *fields, *rims)

    gram = gram + lax.ppermute(gram, "dom", [(i, i ^ 1) for i in range(count)])
    grams = from_all(gram, "dom", [list(range(core, count, 2)) for core in range(2)])

    low_sum, own_sum, high_sum, eig_deriv = pl.pallas_call(
        functools.partial(energy_kernel, modes, groups, nodes, des, elems),
        in_specs=[vmem] * (7 + 2 * groups),
        out_specs=[vmem] * 4,
        out_shape=[shaped((1, des), f32)] * 3 + [shaped((1, modes), f32)],
        scratch_shapes=[
            pltpu.VMEM((rows, nodes + LANES), bf16),
            pltpu.VMEM((modes, LANES), f32),
            pltpu.VMEM((nodes + LANES, wide), bf16),
            pltpu.VMEM((entries, LANES), f32),
        ],
        compiler_params=params(24),
        name="energy",
    )(grams, eig_copy, weight_copy, *fields, *rims, conn, owner_row, resid, power)

    owned = own_sum + neighbour(low_sum, -1) + neighbour(high_sum, 1)
    hess_vec = jnp.sum(from_all(owned, "mode", [list(range(groups))]), axis=0)
    return (hess_vec.reshape(des), eig_deriv.reshape(modes))


def solution(mesh):
    return jax.shard_map(
        on_device,
        mesh=mesh,
        in_specs=(
            P("mode", None, "dom"),
            P(),
            P("mode"),
            P(None, None, "dom"),
            P(),
            P("dom"),
            P(None, "dom"),
            P("dom"),
            P("dom"),
        ),
        out_specs=(P("dom"), P("mode")),
        check_vma=False,
    )
```

```python
import functools

import jax
import jax.numpy as jnp
from jax import lax
from jax.experimental import pallas as pl
from jax.experimental.pallas import tpu as pltpu
from jax.sharding import PartitionSpec as P

H = 32
COMPS = 6
CORNERS = 4
DOFS = 24
TILE = 768
LANES = 128
EXTRA = 16
SUBS = 8
MIB = 1 << 20
f32, bf16 = jnp.float32, jnp.bfloat16


def dot(a, b):
    return lax.dot_general(a, b, (((1,), (0,)), ((), ())), preferred_element_type=f32)


def dot_nt(a, b):
    return lax.dot_general(a, b, (((1,), (1,)), ((), ())), preferred_element_type=f32)


def iota(shape, dim):
    return lax.broadcasted_iota(jnp.int32, shape, dim)


def one_hot(rows, index):
    hit = iota((rows, index.shape[1]), 0) == index
    return jnp.where(hit, 1.0, 0.0).astype(bf16)


def three_pieces(x):
    first = x.astype(bf16)
    rest = x - first.astype(f32)
    second = rest.astype(bf16)
    third = (rest - second.astype(f32)).astype(bf16)
    return first, second, third


def column_of(row, offset, count):
    n = row.shape[1]
    mask = iota((count, n), 1) == iota((count, n), 0) + offset
    return jnp.sum(jnp.where(mask, row, 0.0), axis=1, keepdims=True)


def pack_kernel(rows, des, first_ref, last_ref, dir_ref, up_ref, down_ref):
    up_ref[0:rows, :] = last_ref[...]
    down_ref[0:rows, :] = first_ref[...]
    table = jnp.concatenate(
        [dir_ref[i * LANES : (i + 1) * LANES].reshape(1, LANES) for i in range(des // LANES)], axis=0
    )
    pieces = [p.astype(f32) for p in three_pieces(table)]
    pad = jnp.zeros((EXTRA - 3 * (des // LANES), LANES), f32)
    packed = jnp.concatenate(pieces + [pad], axis=0).astype(bf16)
    up_ref[rows : rows + EXTRA, :] = packed
    down_ref[rows : rows + EXTRA, :] = packed


def fill_one_hot(conn_ref, at, hot, nodes):
    for k in range(CORNERS):
        index = conn_ref[k : k + 1, pl.ds(at, TILE)]
        index = jnp.where(index < H, index + (nodes + LANES - H), index - H)
        hot[:, k * TILE : (k + 1) * TILE] = one_hot(nodes + LANES, index)


def rows_of(flat_ref, row_ref):
    for i in range(row_ref.shape[1] // LANES):
        span = slice(i * LANES, (i + 1) * LANES)
        row_ref[:, span] = flat_ref[span].reshape(1, LANES)


def expand_mass(ref):
    size = DOFS * SUBS
    spread = jnp.where(iota((size, DOFS), 0) // SUBS == iota((size, DOFS), 1), 1.0, 0.0).astype(bf16)
    full = dot_nt(dot(spread, ref).astype(bf16), spread)
    same = iota((size, size), 0) % SUBS == iota((size, size), 1) % SUBS
    return jnp.where(same, full, 0.0).astype(bf16)


def forces_kernel(
    modes,
    nodes,
    des,
    elems,
    conn_hbm,
    owner_hbm,
    mass_hbm,
    stiff_hbm,
    field_hbm,
    ref_hbm,
    eig_hbm,
    weight_hbm,
    own_hbm,
    low_ref,
    high_ref,
    resid_ref,
    power_ref,
    node_ref,
    conn,
    owner_row,
    eig_row,
    weight_row,
    owner_flat,
    mass_flat,
    stiff,
    field,
    ref,
    own,
    sems,
    stiff_sems,
    mass_row,
    dir_row,
    mass_big,
    hot,
    shapes,
    mass_q,
    stiff_wide,
    force,
    sums_t,
):
    rows = COMPS * modes
    tiles = elems // TILE
    rank = lax.axis_index("dom")
    mode_start = lax.axis_index("mode") * modes
    entries = 16
    small = [
        pltpu.make_async_copy(source, target, sems.at[i])
        for i, (source, target) in enumerate(
            (
                (ref_hbm, ref),
                (conn_hbm, conn),
                (field_hbm, field.at[:, pl.ds(0, nodes)]),
                (owner_hbm, owner_flat),
                (mass_hbm, mass_flat),
                (eig_hbm, eig_row),
                (weight_hbm, weight_row),
                (own_hbm.at[pl.ds(rows, EXTRA)], own),
            )
        )
    ]

    def stiff_copy(t):
        cols = pl.ds(pl.multiple_of(t * TILE, TILE), TILE)
        return pltpu.make_async_copy(stiff_hbm.at[:, :, cols], stiff.at[t], stiff_sems.at[t])

    for copy in small:
        copy.start()
    for t in range(tiles):
        stiff_copy(t).start()

    lower = iota((rows, LANES), 1) >= LANES // 2
    field[:, nodes : nodes + LANES] = jnp.where(
        lower, low_ref[0:rows, :].astype(f32), high_ref[0:rows, :].astype(f32)
    ).astype(bf16)
    sums_t[...] = jnp.zeros_like(sums_t)
    for copy in small:
        copy.wait()
    per = des // LANES
    sides = []
    for pieces in (low_ref[rows : rows + EXTRA, :], own[...], high_ref[rows : rows + EXTRA, :]):
        packed = pieces.astype(f32)
        sides.append(packed[:per] + packed[per : 2 * per] + packed[2 * per : 3 * per])
    sides.append(jnp.zeros((entries - 3 * per, LANES), f32))
    table = jnp.concatenate(three_pieces(jnp.concatenate(sides, axis=0)), axis=0)
    mass_big[...] = expand_mass(ref[...])
    rows_of(owner_flat, owner_row)
    rows_of(mass_flat, mass_row)
    eig = column_of(eig_row[...], mode_start, modes)
    weight = 2.0 * column_of(weight_row[...], 0, modes)
    local = owner_row[...] - (rank - 1) * des
    looked = dot(table, one_hot(LANES, local % LANES))
    looked = looked[:entries] + looked[entries : 2 * entries] + looked[2 * entries :]
    here = iota((entries, elems), 0) == local // LANES
    dir_row[...] = jnp.sum(jnp.where(here, looked, 0.0), axis=0, keepdims=True)

    @pl.loop(0, tiles)
    def _(t):
        at = pl.multiple_of(t * TILE, TILE)
        elem_dir = dir_row[:, pl.ds(at, TILE)]
        elem_mass = mass_row[:, pl.ds(at, TILE)]
        fill_one_hot(conn, at, hot, nodes)
        shapes[...] = dot(field[...], hot[...])
        for g in range(modes // SUBS):
            stacked = [
                shapes[
                    (b // CORNERS) * modes + g * SUBS : (b // CORNERS) * modes + (g + 1) * SUBS,
                    (b % CORNERS) * TILE : (b % CORNERS + 1) * TILE,
                ]
                for b in range(DOFS)
            ]
            mass_q[g] = dot(mass_big[...], jnp.concatenate(stacked, axis=0).astype(bf16))
        stiff_copy(t).wait()
        stiff_wide[...] = stiff[t].astype(f32)

        for lane in range(TILE // LANES):
            cols = slice(lane * LANES, (lane + 1) * LANES)
            at_lane = pl.multiple_of(at + lane * LANES, LANES)
            direction = elem_dir[:, cols]
            mass = elem_mass[:, cols]
            scaled = eig * mass
            dir_mass = direction * mass
            power = jnp.zeros((modes, LANES), f32)
            for first in range(0, DOFS, 4):
                sums = [jnp.zeros((modes, LANES), f32) for _ in range(4)]
                for b in range(DOFS):
                    c, k = b // CORNERS, b % CORNERS
                    col = k * TILE + lane * LANES
                    s = shapes[c * modes : (c + 1) * modes, col : col + LANES]
                    for q in range(4):
                        sums[q] = sums[q] + stiff_wide[first + q, b : b + 1, cols] * s
                for q in range(4):
                    c, k = (first + q) // CORNERS, (first + q) % CORNERS
                    col = k * TILE + lane * LANES
                    s = shapes[c * modes : (c + 1) * modes, col : col + LANES]
                    base = k * rows + c * modes
                    mq = jnp.concatenate(
                        [
                            mass_q[g, (first + q) * SUBS : (first + q + 1) * SUBS, cols]
                            for g in range(modes // SUBS)
                        ],
                        axis=0,
                    )
                    power = power + s * mq
                    span = slice(c * modes, (c + 1) * modes)
                    force[span, col : col + LANES] = (direction * sums[q]).astype(bf16)
                    span = slice(rows + c * modes, rows + (c + 1) * modes)
                    force[span, col : col + LANES] = (dir_mass * mq).astype(bf16)
                    resid_ref[base : base + modes, pl.ds(at_lane, LANES)] = weight * (
                        sums[q] - scaled * mq
                    )
            power_ref[:, pl.ds(at_lane, LANES)] = power * mass

        sums_t[...] += dot_nt(hot[...], force[...])

    for i in range((nodes + LANES) // LANES):
        span = slice(i * LANES, (i + 1) * LANES)
        for part in range(2 * rows // LANES):
            node_ref[part * LANES : (part + 1) * LANES, span] = sums_t[
                span, part * LANES : (part + 1) * LANES
            ].T


def gather_modes(refs, c, modes):
    return jnp.concatenate([r[c * modes : (c + 1) * modes, :] for r in refs], axis=0)


def gram_kernel(modes, groups, nodes, node_ref, eig_ref, *refs):
    fields, rims, out_ref = refs[:groups], refs[groups : 2 * groups], refs[2 * groups]
    rows = COMPS * modes
    eig = column_of(eig_ref[...], lax.axis_index("mode") * modes, modes)
    grams = [jnp.zeros((modes, groups * modes), f32) for _ in range(2)]
    for c in range(COMPS):
        for cols, parts in ((slice(0, nodes), fields), (slice(nodes, nodes + LANES), rims)):
            pieces = []
            for kind in range(2):
                base = kind * rows + c * modes
                pieces += three_pieces(node_ref[base : base + modes, cols])
            each = dot_nt(jnp.concatenate(pieces, axis=0), gather_modes(parts, c, modes))
            each = [each[i * modes : (i + 1) * modes] for i in range(6)]
            grams = [grams[k] + (each[3 * k] + (each[3 * k + 1] + each[3 * k + 2])) for k in range(2)]
    stiff_gram, mass_gram = grams
    out_ref[0:modes, :] = stiff_gram - eig * mass_gram
    mask = iota(mass_gram.shape, 0) == iota(mass_gram.shape, 1)
    out_ref[modes : modes + 8, :] = jnp.broadcast_to(
        jnp.sum(jnp.where(mask, mass_gram, 0.0), axis=0, keepdims=True), (8, LANES)
    )


def energy_kernel(modes, groups, nodes, des, elems, gram_ref, eig_ref, weight_ref, *refs):
    fields, rims, refs = refs[:groups], refs[groups : 2 * groups], refs[2 * groups :]
    conn_ref, owner_row, resid_ref, power_ref = refs[:4]
    low_ref, own_ref, high_ref, deriv_ref = refs[4:8]
    deriv, factor, hot, totals = refs[8:]
    rows = COMPS * modes
    rank = lax.axis_index("dom")
    mode_start = lax.axis_index("mode") * modes

    total = gram_ref[0]
    for i in range(1, gram_ref.shape[0]):
        total = total + gram_ref[i]
    gram = total[:modes]
    mass_diag = column_of(total[modes : modes + 1], 0, modes)
    shape = (modes, groups * modes)
    mask = iota(shape, 0) == iota(shape, 1)
    eig_rows = jnp.broadcast_to(eig_ref[...], (8, LANES))
    turned = pltpu.roll(eig_rows, lax.rem(LANES - mode_start, LANES), 1)[0:1]
    spacing = column_of(turned, 0, modes) - turned
    combiner = jnp.where(mask, -0.5 * mass_diag, gram / jnp.where(mask, 1.0, spacing)).astype(bf16)
    diagonal = jnp.where(mask, gram, 0.0)
    deriv_ref[...] = jnp.sum(diagonal, axis=0, keepdims=True)[:, :modes]
    eig_deriv = jnp.sum(diagonal, axis=1, keepdims=True)
    factor[...] = jnp.broadcast_to(eig_deriv * column_of(weight_ref[...], 0, modes), factor.shape)
    for c in range(COMPS):
        span = slice(c * modes, (c + 1) * modes)
        deriv[span, 0:nodes] = dot(combiner, gather_modes(fields, c, modes)).astype(bf16)
        deriv[span, nodes : nodes + LANES] = dot(combiner, gather_modes(rims, c, modes)).astype(bf16)
    totals[...] = jnp.zeros_like(totals)

    @pl.loop(0, elems // TILE)
    def _(t):
        at = pl.multiple_of(t * TILE, TILE)
        fill_one_hot(conn_ref, at, hot, nodes)
        moved = dot(deriv[...], hot[...])
        energies = []
        for lane in range(TILE // LANES):
            cols = pl.ds(pl.multiple_of(at + lane * LANES, LANES), LANES)
            total = -factor[...] * power_ref[:, cols]
            for k in range(CORNERS):
                col = k * TILE + lane * LANES
                for c in range(COMPS):
                    base = k * rows + c * modes
                    total = total + moved[
                        c * modes : (c + 1) * modes, col : col + LANES
                    ] * resid_ref[base : base + modes, cols]
            energies.append(jnp.sum(total, axis=0, keepdims=True))
        energy = jnp.concatenate(energies, axis=1)
        local = owner_row[:, pl.ds(at, TILE)] - (rank - 1) * des
        entries = totals.shape[0]
        here = iota((entries, TILE), 0) == local // LANES
        spread = jnp.concatenate(
            [jnp.where(here, p.astype(f32), 0.0).astype(bf16) for p in three_pieces(energy)], axis=0
        )
        sums = dot_nt(spread, one_hot(LANES, local % LANES))
        totals[...] += sums[:entries] + sums[entries : 2 * entries] + sums[2 * entries :]

    per = des // LANES
    for side, ref in enumerate((low_ref, own_ref, high_ref)):
        for i in range(per):
            at = side * per + i
            ref[:, i * LANES : (i + 1) * LANES] = totals[at : at + 1, :]


def neighbour(value, step):
    count = lax.axis_size("dom")
    pairs = [(i, i + step) for i in range(count) if 0 <= i + step < count]
    return lax.ppermute(value, "dom", pairs)


def shift_in(value, axis, step):
    count = lax.axis_size(axis)
    return lax.ppermute(value, axis, [(i, (i - step) % count) for i in range(count)])


def from_all(value, axis, groups):
    size = len(groups[0])
    copies = jnp.broadcast_to(value[None], (size,) + value.shape)
    return lax.all_to_all(copies, axis, 0, 0, axis_index_groups=groups)


def whole(shape):
    return pl.BlockSpec(shape, lambda t: (0,) * len(shape))


def params(mib):
    return pltpu.CompilerParams(vmem_limit_bytes=mib * MIB)


def cost(flops, bytes_):
    return pl.CostEstimate(flops=flops, bytes_accessed=bytes_, transcendentals=0)


def on_device(
    mode_shapes,
    eigenvalues,
    mode_weights,
    stiff_deriv,
    mass_ref,
    mass_scale,
    connectivity,
    design_owner,
    direction,
):
    modes, _, nodes = mode_shapes.shape
    elems = connectivity.shape[1]
    des = direction.shape[0]
    groups = lax.axis_size("mode")
    count = lax.axis_size("dom")
    total_modes = groups * modes
    rows = COMPS * modes
    big = CORNERS * rows
    tiles = elems // TILE
    wide = CORNERS * TILE
    entries = 16
    shaped = jax.ShapeDtypeStruct
    vmem = pl.BlockSpec(memory_space=pltpu.VMEM)
    hbm = pl.BlockSpec(memory_space=pltpu.HBM)

    field = jnp.transpose(mode_shapes, (1, 0, 2)).reshape(rows, nodes)
    eig_row = eigenvalues.reshape(1, total_modes)
    weight_row = mode_weights.reshape(1, modes)

    up, down = pl.pallas_call(
        functools.partial(pack_kernel, rows, des),
        grid=(1,),
        in_specs=[
            pl.BlockSpec((rows, LANES), lambda t: (0, 0)),
            pl.BlockSpec((rows, LANES), lambda t: (0, nodes // LANES - 1)),
            whole((des,)),
        ],
        out_specs=[whole((rows + EXTRA, LANES))] * 2,
        out_shape=[shaped((rows + EXTRA, LANES), bf16)] * 2,
        name="pack",
    )(field, field, direction)
    sent, up, down = lax.optimization_barrier((field, up, down))
    low, high = neighbour(up, 1), neighbour(down, -1)
    upper = lax.broadcasted_iota(jnp.int32, (rows, LANES), 1) < LANES // 2
    rim = jnp.where(upper, high[:rows], low[:rows])
    fields = [field] + [shift_in(sent, "mode", s) for s in range(1, groups)]
    rims = [rim] + [shift_in(rim, "mode", s) for s in range(1, groups)]

    def pinned(*values):
        return [pltpu.with_memory_space_constraint(v, pltpu.HBM) for v in values]

    resid, power, node, conn, owner_row, eig_copy, weight_copy = pl.pallas_call(
        functools.partial(forces_kernel, modes, nodes, des, elems),
        in_specs=[hbm] * 9 + [vmem] * 2,
        out_specs=[vmem] * 7,
        out_shape=[
            shaped((big, elems), f32),
            shaped((modes, elems), f32),
            shaped((2 * rows, nodes + LANES), f32),
            shaped((CORNERS, elems), jnp.int32),
            shaped((1, elems), jnp.int32),
            shaped((1, total_modes), f32),
            shaped((1, modes), f32),
        ],
        scratch_shapes=[
            pltpu.VMEM((elems,), jnp.int32),
            pltpu.VMEM((elems,), f32),
            pltpu.VMEM((tiles, DOFS, DOFS, TILE), bf16),
            pltpu.VMEM((rows, nodes + LANES), bf16),
            pltpu.VMEM((DOFS, DOFS), bf16),
            pltpu.VMEM((EXTRA, LANES), bf16),
            pltpu.SemaphoreType.DMA((8,)),
            pltpu.SemaphoreType.DMA((tiles,)),
            pltpu.VMEM((1, elems), f32),
            pltpu.VMEM((1, elems), f32),
            pltpu.VMEM((DOFS * SUBS, DOFS * SUBS), bf16),
            pltpu.VMEM((nodes + LANES, wide), bf16),
            pltpu.VMEM((rows, wide), f32),
            pltpu.VMEM((modes // SUBS, DOFS * SUBS, TILE), f32),
            pltpu.VMEM((DOFS, DOFS, TILE), f32),
            pltpu.VMEM((2 * rows, wide), bf16),
            pltpu.VMEM((nodes + LANES, 2 * rows), f32),
        ],
        compiler_params=params(44),
        cost_estimate=cost(1_000_000, 100_000),
        name="forces",
    )(
        *pinned(
            connectivity,
            design_owner,
            mass_scale,
            stiff_deriv,
            field,
            mass_ref,
            eig_row,
            weight_row,
            up,
        ),
        low,
        high,
    )

    gram = pl.pallas_call(
        functools.partial(gram_kernel, modes, groups, nodes),
        out_shape=shaped((modes + 8, total_modes), f32),
        compiler_params=params(24),
        name="gram",
    )(node, eig_copy, *fields, *rims)

    gram = gram + lax.ppermute(gram, "dom", [(i, i ^ 1) for i in range(count)])
    grams = from_all(gram, "dom", [list(range(core, count, 2)) for core in range(2)])

    low_sum, own_sum, high_sum, eig_deriv = pl.pallas_call(
        functools.partial(energy_kernel, modes, groups, nodes, des, elems),
        in_specs=[vmem] * (7 + 2 * groups),
        out_specs=[vmem] * 4,
        out_shape=[shaped((1, des), f32)] * 3 + [shaped((1, modes), f32)],
        scratch_shapes=[
            pltpu.VMEM((rows, nodes + LANES), bf16),
            pltpu.VMEM((modes, LANES), f32),
            pltpu.VMEM((nodes + LANES, wide), bf16),
            pltpu.VMEM((entries, LANES), f32),
        ],
        compiler_params=params(44),
        name="energy",
    )(grams, eig_copy, weight_copy, *fields, *rims, conn, owner_row, resid, power)

    owned = own_sum + neighbour(low_sum, -1) + neighbour(high_sum, 1)
    hess_vec = jnp.sum(from_all(owned, "mode", [list(range(groups))]), axis=0)
    return (hess_vec.reshape(des), eig_deriv.reshape(modes))


def solution(mesh):
    return jax.shard_map(
        on_device,
        mesh=mesh,
        in_specs=(
            P("mode", None, "dom"),
            P(),
            P("mode"),
            P(None, None, "dom"),
            P(),
            P("dom"),
            P(None, "dom"),
            P("dom"),
            P("dom"),
        ),
        out_specs=(P("dom"), P("mode")),
        check_vma=False,
    )
```

```python
import functools

import jax
import jax.numpy as jnp
from jax import lax
from jax.experimental import pallas as pl
from jax.experimental.pallas import tpu as pltpu
from jax.sharding import PartitionSpec as P

H = 32
COMPS = 6
CORNERS = 4
DOFS = 24
TILE = 768
LANES = 128
EXTRA = 16
SUBS = 8
MIB = 1 << 20
f32, bf16 = jnp.float32, jnp.bfloat16


def dot(a, b):
    return lax.dot_general(a, b, (((1,), (0,)), ((), ())), preferred_element_type=f32)


def dot_nt(a, b):
    return lax.dot_general(a, b, (((1,), (1,)), ((), ())), preferred_element_type=f32)


def iota(shape, dim):
    return lax.broadcasted_iota(jnp.int32, shape, dim)


def one_hot(rows, index):
    hit = iota((rows, index.shape[1]), 0) == index
    return jnp.where(hit, 1.0, 0.0).astype(bf16)


def three_pieces(x):
    first = x.astype(bf16)
    rest = x - first.astype(f32)
    second = rest.astype(bf16)
    third = (rest - second.astype(f32)).astype(bf16)
    return first, second, third


def column_of(row, offset, count):
    n = row.shape[1]
    mask = iota((count, n), 1) == iota((count, n), 0) + offset
    return jnp.sum(jnp.where(mask, row, 0.0), axis=1, keepdims=True)


def pack_kernel(rows, des, first_ref, last_ref, dir_ref, up_ref, down_ref):
    up_ref[0:rows, :] = last_ref[...]
    down_ref[0:rows, :] = first_ref[...]
    table = jnp.concatenate(
        [dir_ref[i * LANES : (i + 1) * LANES].reshape(1, LANES) for i in range(des // LANES)], axis=0
    )
    pieces = [p.astype(f32) for p in three_pieces(table)]
    pad = jnp.zeros((EXTRA - 3 * (des // LANES), LANES), f32)
    packed = jnp.concatenate(pieces + [pad], axis=0).astype(bf16)
    up_ref[rows : rows + EXTRA, :] = packed
    down_ref[rows : rows + EXTRA, :] = packed


def fill_one_hot(conn_ref, at, hot, nodes):
    for k in range(CORNERS):
        index = conn_ref[k : k + 1, pl.ds(at, TILE)]
        index = jnp.where(index < H, index + (nodes + LANES - H), index - H)
        hot[:, k * TILE : (k + 1) * TILE] = one_hot(nodes + LANES, index)


def rows_of(flat_ref, row_ref):
    for i in range(row_ref.shape[1] // LANES):
        span = slice(i * LANES, (i + 1) * LANES)
        row_ref[:, span] = flat_ref[span].reshape(1, LANES)


def expand_mass(ref):
    size = DOFS * SUBS
    spread = jnp.where(iota((size, DOFS), 0) // SUBS == iota((size, DOFS), 1), 1.0, 0.0).astype(bf16)
    full = dot_nt(dot(spread, ref).astype(bf16), spread)
    same = iota((size, size), 0) % SUBS == iota((size, size), 1) % SUBS
    return jnp.where(same, full, 0.0).astype(bf16)


def forces_kernel(
    modes,
    nodes,
    des,
    elems,
    conn_hbm,
    owner_hbm,
    mass_hbm,
    stiff_hbm,
    ref_hbm,
    eig_hbm,
    weight_hbm,
    own_hbm,
    field,
    low_ref,
    high_ref,
    resid_ref,
    power_ref,
    node_ref,
    conn,
    owner_row,
    eig_row,
    weight_row,
    owner_flat,
    mass_flat,
    stiff,
    ref,
    own,
    sems,
    stiff_sems,
    mass_row,
    dir_row,
    mass_big,
    hot,
    shapes,
    mass_q,
    stiff_wide,
    force,
    sums_t,
):
    rows = COMPS * modes
    tiles = elems // TILE
    rank = lax.axis_index("dom")
    mode_start = lax.axis_index("mode") * modes
    entries = 16
    small = [
        pltpu.make_async_copy(source, target, sems.at[i])
        for i, (source, target) in enumerate(
            (
                (ref_hbm, ref),
                (conn_hbm, conn),
                (owner_hbm, owner_flat),
                (mass_hbm, mass_flat),
                (eig_hbm, eig_row),
                (weight_hbm, weight_row),
                (own_hbm.at[pl.ds(rows, EXTRA)], own),
            )
        )
    ]

    def stiff_copy(t):
        cols = pl.ds(pl.multiple_of(t * TILE, TILE), TILE)
        return pltpu.make_async_copy(stiff_hbm.at[:, :, cols], stiff.at[t], stiff_sems.at[t])

    for copy in small:
        copy.start()
    for t in range(tiles):
        stiff_copy(t).start()

    sums_t[...] = jnp.zeros_like(sums_t)
    for copy in small:
        copy.wait()
    per = des // LANES
    sides = []
    for pieces in (low_ref[rows : rows + EXTRA, :], own[...], high_ref[rows : rows + EXTRA, :]):
        packed = pieces.astype(f32)
        sides.append(packed[:per] + packed[per : 2 * per] + packed[2 * per : 3 * per])
    sides.append(jnp.zeros((entries - 3 * per, LANES), f32))
    table = jnp.concatenate(three_pieces(jnp.concatenate(sides, axis=0)), axis=0)
    mass_big[...] = expand_mass(ref[...])
    rows_of(owner_flat, owner_row)
    rows_of(mass_flat, mass_row)
    eig = column_of(eig_row[...], mode_start, modes)
    weight = 2.0 * column_of(weight_row[...], 0, modes)
    local = owner_row[...] - (rank - 1) * des
    looked = dot(table, one_hot(LANES, local % LANES))
    looked = looked[:entries] + looked[entries : 2 * entries] + looked[2 * entries :]
    here = iota((entries, elems), 0) == local // LANES
    dir_row[...] = jnp.sum(jnp.where(here, looked, 0.0), axis=0, keepdims=True)

    @pl.loop(0, tiles)
    def _(t):
        at = pl.multiple_of(t * TILE, TILE)
        elem_dir = dir_row[:, pl.ds(at, TILE)]
        elem_mass = mass_row[:, pl.ds(at, TILE)]
        fill_one_hot(conn, at, hot, nodes)
        shapes[...] = dot(field[...], hot[...])
        for g in range(modes // SUBS):
            stacked = [
                shapes[
                    (b // CORNERS) * modes + g * SUBS : (b // CORNERS) * modes + (g + 1) * SUBS,
                    (b % CORNERS) * TILE : (b % CORNERS + 1) * TILE,
                ]
                for b in range(DOFS)
            ]
            mass_q[g] = dot(mass_big[...], jnp.concatenate(stacked, axis=0).astype(bf16))
        stiff_copy(t).wait()
        stiff_wide[...] = stiff[t].astype(f32)

        for lane in range(TILE // LANES):
            cols = slice(lane * LANES, (lane + 1) * LANES)
            at_lane = pl.multiple_of(at + lane * LANES, LANES)
            direction = elem_dir[:, cols]
            mass = elem_mass[:, cols]
            scaled = eig * mass
            dir_mass = direction * mass
            power = jnp.zeros((modes, LANES), f32)
            for first in range(0, DOFS, 4):
                sums = [jnp.zeros((modes, LANES), f32) for _ in range(4)]
                for b in range(DOFS):
                    c, k = b // CORNERS, b % CORNERS
                    col = k * TILE + lane * LANES
                    s = shapes[c * modes : (c + 1) * modes, col : col + LANES]
                    for q in range(4):
                        sums[q] = sums[q] + stiff_wide[first + q, b : b + 1, cols] * s
                for q in range(4):
                    c, k = (first + q) // CORNERS, (first + q) % CORNERS
                    col = k * TILE + lane * LANES
                    s = shapes[c * modes : (c + 1) * modes, col : col + LANES]
                    base = k * rows + c * modes
                    mq = jnp.concatenate(
                        [
                            mass_q[g, (first + q) * SUBS : (first + q + 1) * SUBS, cols]
                            for g in range(modes // SUBS)
                        ],
                        axis=0,
                    )
                    power = power + s * mq
                    span = slice(c * modes, (c + 1) * modes)
                    force[span, col : col + LANES] = (direction * sums[q]).astype(bf16)
                    span = slice(rows + c * modes, rows + (c + 1) * modes)
                    force[span, col : col + LANES] = (dir_mass * mq).astype(bf16)
                    resid_ref[base : base + modes, pl.ds(at_lane, LANES)] = weight * (
                        sums[q] - scaled * mq
                    )
            power_ref[:, pl.ds(at_lane, LANES)] = power * mass

        sums_t[...] += dot_nt(hot[...], force[...])

    for i in range((nodes + LANES) // LANES):
        span = slice(i * LANES, (i + 1) * LANES)
        for part in range(2 * rows // LANES):
            node_ref[part * LANES : (part + 1) * LANES, span] = sums_t[
                span, part * LANES : (part + 1) * LANES
            ].T


def gather_modes(refs, c, modes):
    return jnp.concatenate([r[c * modes : (c + 1) * modes, :] for r in refs], axis=0)


def gram_kernel(modes, groups, node_ref, eig_ref, *refs):
    fields, out_ref = refs[:groups], refs[groups]
    rows = COMPS * modes
    eig = column_of(eig_ref[...], lax.axis_index("mode") * modes, modes)
    grams = [jnp.zeros((modes, groups * modes), f32) for _ in range(2)]
    for c in range(COMPS):
        pieces = []
        for kind in range(2):
            base = kind * rows + c * modes
            pieces += three_pieces(node_ref[base : base + modes, :])
        each = dot_nt(jnp.concatenate(pieces, axis=0), gather_modes(fields, c, modes))
        each = [each[i * modes : (i + 1) * modes] for i in range(6)]
        grams = [grams[k] + (each[3 * k] + (each[3 * k + 1] + each[3 * k + 2])) for k in range(2)]
    stiff_gram, mass_gram = grams
    out_ref[0:modes, :] = stiff_gram - eig * mass_gram
    mask = iota(mass_gram.shape, 0) == iota(mass_gram.shape, 1)
    out_ref[modes : modes + 8, :] = jnp.broadcast_to(
        jnp.sum(jnp.where(mask, mass_gram, 0.0), axis=0, keepdims=True), (8, LANES)
    )


def energy_kernel(modes, groups, nodes, des, elems, gram_ref, eig_ref, weight_ref, *refs):
    fields, refs = refs[:groups], refs[groups:]
    conn_ref, owner_row, resid_ref, power_ref = refs[:4]
    low_ref, own_ref, high_ref, deriv_ref = refs[4:8]
    deriv, factor, hot, totals = refs[8:]
    rows = COMPS * modes
    rank = lax.axis_index("dom")
    mode_start = lax.axis_index("mode") * modes

    total = gram_ref[0]
    for i in range(1, gram_ref.shape[0]):
        total = total + gram_ref[i]
    gram = total[:modes]
    mass_diag = column_of(total[modes : modes + 1], 0, modes)
    shape = (modes, groups * modes)
    mask = iota(shape, 0) == iota(shape, 1)
    eig_rows = jnp.broadcast_to(eig_ref[...], (8, LANES))
    turned = pltpu.roll(eig_rows, lax.rem(LANES - mode_start, LANES), 1)[0:1]
    spacing = column_of(turned, 0, modes) - turned
    combiner = jnp.where(mask, -0.5 * mass_diag, gram / jnp.where(mask, 1.0, spacing)).astype(bf16)
    diagonal = jnp.where(mask, gram, 0.0)
    deriv_ref[...] = jnp.sum(diagonal, axis=0, keepdims=True)[:, :modes]
    eig_deriv = jnp.sum(diagonal, axis=1, keepdims=True)
    factor[...] = jnp.broadcast_to(eig_deriv * column_of(weight_ref[...], 0, modes), factor.shape)
    for c in range(COMPS):
        span = slice(c * modes, (c + 1) * modes)
        deriv[span, :] = dot(combiner, gather_modes(fields, c, modes)).astype(bf16)
    totals[...] = jnp.zeros_like(totals)

    @pl.loop(0, elems // TILE)
    def _(t):
        at = pl.multiple_of(t * TILE, TILE)
        fill_one_hot(conn_ref, at, hot, nodes)
        moved = dot(deriv[...], hot[...])
        energies = []
        for lane in range(TILE // LANES):
            cols = pl.ds(pl.multiple_of(at + lane * LANES, LANES), LANES)
            total = -factor[...] * power_ref[:, cols]
            for k in range(CORNERS):
                col = k * TILE + lane * LANES
                for c in range(COMPS):
                    base = k * rows + c * modes
                    total = total + moved[
                        c * modes : (c + 1) * modes, col : col + LANES
                    ] * resid_ref[base : base + modes, cols]
            energies.append(jnp.sum(total, axis=0, keepdims=True))
        energy = jnp.concatenate(energies, axis=1)
        local = owner_row[:, pl.ds(at, TILE)] - (rank - 1) * des
        entries = totals.shape[0]
        here = iota((entries, TILE), 0) == local // LANES
        spread = jnp.concatenate(
            [jnp.where(here, p.astype(f32), 0.0).astype(bf16) for p in three_pieces(energy)], axis=0
        )
        sums = dot_nt(spread, one_hot(LANES, local % LANES))
        totals[...] += sums[:entries] + sums[entries : 2 * entries] + sums[2 * entries :]

    per = des // LANES
    for side, ref in enumerate((low_ref, own_ref, high_ref)):
        for i in range(per):
            at = side * per + i
            ref[:, i * LANES : (i + 1) * LANES] = totals[at : at + 1, :]


def neighbour(value, step):
    count = lax.axis_size("dom")
    pairs = [(i, i + step) for i in range(count) if 0 <= i + step < count]
    return lax.ppermute(value, "dom", pairs)


def shift_in(value, axis, step):
    count = lax.axis_size(axis)
    return lax.ppermute(value, axis, [(i, (i - step) % count) for i in range(count)])


def from_all(value, axis, groups):
    size = len(groups[0])
    copies = jnp.broadcast_to(value[None], (size,) + value.shape)
    return lax.all_to_all(copies, axis, 0, 0, axis_index_groups=groups)


def whole(shape):
    return pl.BlockSpec(shape, lambda t: (0,) * len(shape))


def params(mib):
    return pltpu.CompilerParams(vmem_limit_bytes=mib * MIB)


def cost(flops, bytes_):
    return pl.CostEstimate(flops=flops, bytes_accessed=bytes_, transcendentals=0)


def on_device(
    mode_shapes,
    eigenvalues,
    mode_weights,
    stiff_deriv,
    mass_ref,
    mass_scale,
    connectivity,
    design_owner,
    direction,
):
    modes, _, nodes = mode_shapes.shape
    elems = connectivity.shape[1]
    des = direction.shape[0]
    groups = lax.axis_size("mode")
    count = lax.axis_size("dom")
    total_modes = groups * modes
    rows = COMPS * modes
    big = CORNERS * rows
    tiles = elems // TILE
    wide = CORNERS * TILE
    entries = 16
    shaped = jax.ShapeDtypeStruct
    vmem = pl.BlockSpec(memory_space=pltpu.VMEM)
    hbm = pl.BlockSpec(memory_space=pltpu.HBM)

    field = jnp.transpose(mode_shapes, (1, 0, 2)).reshape(rows, nodes)
    eig_row = eigenvalues.reshape(1, total_modes)
    weight_row = mode_weights.reshape(1, modes)

    up, down = pl.pallas_call(
        functools.partial(pack_kernel, rows, des),
        grid=(1,),
        in_specs=[
            pl.BlockSpec((rows, LANES), lambda t: (0, 0)),
            pl.BlockSpec((rows, LANES), lambda t: (0, nodes // LANES - 1)),
            whole((des,)),
        ],
        out_specs=[whole((rows + EXTRA, LANES))] * 2,
        out_shape=[shaped((rows + EXTRA, LANES), bf16)] * 2,
        name="pack",
    )(field, field, direction)
    low, high = neighbour(up, 1), neighbour(down, -1)
    upper = lax.broadcasted_iota(jnp.int32, (rows, LANES), 1) < LANES // 2
    extended = jnp.concatenate([field, jnp.where(upper, high[:rows], low[:rows])], axis=1)
    fields = [extended] + [shift_in(extended, "mode", s) for s in range(1, groups)]

    def pinned(*values):
        return [pltpu.with_memory_space_constraint(v, pltpu.HBM) for v in values]

    resid, power, node, conn, owner_row, eig_copy, weight_copy = pl.pallas_call(
        functools.partial(forces_kernel, modes, nodes, des, elems),
        in_specs=[hbm] * 8 + [vmem] * 3,
        out_specs=[vmem] * 7,
        out_shape=[
            shaped((big, elems), f32),
            shaped((modes, elems), f32),
            shaped((2 * rows, nodes + LANES), f32),
            shaped((CORNERS, elems), jnp.int32),
            shaped((1, elems), jnp.int32),
            shaped((1, total_modes), f32),
            shaped((1, modes), f32),
        ],
        scratch_shapes=[
            pltpu.VMEM((elems,), jnp.int32),
            pltpu.VMEM((elems,), f32),
            pltpu.VMEM((tiles, DOFS, DOFS, TILE), bf16),
            pltpu.VMEM((DOFS, DOFS), bf16),
            pltpu.VMEM((EXTRA, LANES), bf16),
            pltpu.SemaphoreType.DMA((7,)),
            pltpu.SemaphoreType.DMA((tiles,)),
            pltpu.VMEM((1, elems), f32),
            pltpu.VMEM((1, elems), f32),
            pltpu.VMEM((DOFS * SUBS, DOFS * SUBS), bf16),
            pltpu.VMEM((nodes + LANES, wide), bf16),
            pltpu.VMEM((rows, wide), f32),
            pltpu.VMEM((modes // SUBS, DOFS * SUBS, TILE), f32),
            pltpu.VMEM((DOFS, DOFS, TILE), f32),
            pltpu.VMEM((2 * rows, wide), bf16),
            pltpu.VMEM((nodes + LANES, 2 * rows), f32),
        ],
        compiler_params=params(44),
        cost_estimate=cost(1_000_000, 100_000),
        name="forces",
    )(
        *pinned(
            connectivity,
            design_owner,
            mass_scale,
            stiff_deriv,
            mass_ref,
            eig_row,
            weight_row,
            up,
        ),
        extended,
        low,
        high,
    )

    gram = pl.pallas_call(
        functools.partial(gram_kernel, modes, groups),
        out_shape=shaped((modes + 8, total_modes), f32),
        compiler_params=params(24),
        name="gram",
    )(node, eig_copy, *fields)

    gram = gram + lax.ppermute(gram, "dom", [(i, i ^ 1) for i in range(count)])
    grams = from_all(gram, "dom", [list(range(core, count, 2)) for core in range(2)])

    low_sum, own_sum, high_sum, eig_deriv = pl.pallas_call(
        functools.partial(energy_kernel, modes, groups, nodes, des, elems),
        in_specs=[vmem] * (7 + groups),
        out_specs=[vmem] * 4,
        out_shape=[shaped((1, des), f32)] * 3 + [shaped((1, modes), f32)],
        scratch_shapes=[
            pltpu.VMEM((rows, nodes + LANES), bf16),
            pltpu.VMEM((modes, LANES), f32),
            pltpu.VMEM((nodes + LANES, wide), bf16),
            pltpu.VMEM((entries, LANES), f32),
        ],
        compiler_params=params(44),
        name="energy",
    )(grams, eig_copy, weight_copy, *fields, conn, owner_row, resid, power)

    owned = own_sum + neighbour(low_sum, -1) + neighbour(high_sum, 1)
    hess_vec = jnp.sum(from_all(owned, "mode", [list(range(groups))]), axis=0)
    return (hess_vec.reshape(des), eig_deriv.reshape(modes))


def solution(mesh):
    return jax.shard_map(
        on_device,
        mesh=mesh,
        in_specs=(
            P("mode", None, "dom"),
            P(),
            P("mode"),
            P(None, None, "dom"),
            P(),
            P("dom"),
            P(None, "dom"),
            P("dom"),
            P("dom"),
        ),
        out_specs=(P("dom"), P("mode")),
        check_vma=False,
    )
```

```python
import functools

import jax
import jax.numpy as jnp
from jax import lax
from jax.experimental import pallas as pl
from jax.experimental.pallas import tpu as pltpu
from jax.sharding import PartitionSpec as P

H = 32
COMPS = 6
CORNERS = 4
DOFS = 24
TILE = 768
LANES = 128
EXTRA = 16
SUBS = 8
MIB = 1 << 20
f32, bf16 = jnp.float32, jnp.bfloat16


def dot(a, b):
    return lax.dot_general(a, b, (((1,), (0,)), ((), ())), preferred_element_type=f32)


def dot_nt(a, b):
    return lax.dot_general(a, b, (((1,), (1,)), ((), ())), preferred_element_type=f32)


def iota(shape, dim):
    return lax.broadcasted_iota(jnp.int32, shape, dim)


def one_hot(rows, index):
    hit = iota((rows, index.shape[1]), 0) == index
    return jnp.where(hit, 1.0, 0.0).astype(bf16)


def three_pieces(x):
    first = x.astype(bf16)
    rest = x - first.astype(f32)
    second = rest.astype(bf16)
    third = (rest - second.astype(f32)).astype(bf16)
    return first, second, third


def column_of(row, offset, count):
    n = row.shape[1]
    mask = iota((count, n), 1) == iota((count, n), 0) + offset
    return jnp.sum(jnp.where(mask, row, 0.0), axis=1, keepdims=True)


def pack_kernel(rows, des, first_ref, last_ref, dir_ref, up_ref, down_ref):
    up_ref[0:rows, :] = last_ref[...]
    down_ref[0:rows, :] = first_ref[...]
    table = jnp.concatenate(
        [dir_ref[i * LANES : (i + 1) * LANES].reshape(1, LANES) for i in range(des // LANES)], axis=0
    )
    pieces = [p.astype(f32) for p in three_pieces(table)]
    pad = jnp.zeros((EXTRA - 3 * (des // LANES), LANES), f32)
    packed = jnp.concatenate(pieces + [pad], axis=0).astype(bf16)
    up_ref[rows : rows + EXTRA, :] = packed
    down_ref[rows : rows + EXTRA, :] = packed


def fill_one_hot(conn_ref, at, hot, nodes):
    for k in range(CORNERS):
        index = conn_ref[k : k + 1, pl.ds(at, TILE)]
        index = jnp.where(index < H, index + (nodes + LANES - H), index - H)
        hot[:, k * TILE : (k + 1) * TILE] = one_hot(nodes + LANES, index)


def rows_of(flat_ref, row_ref):
    for i in range(row_ref.shape[1] // LANES):
        span = slice(i * LANES, (i + 1) * LANES)
        row_ref[:, span] = flat_ref[span].reshape(1, LANES)


def expand_mass(ref):
    size = DOFS * SUBS
    spread = jnp.where(iota((size, DOFS), 0) // SUBS == iota((size, DOFS), 1), 1.0, 0.0).astype(bf16)
    full = dot_nt(dot(spread, ref).astype(bf16), spread)
    same = iota((size, size), 0) % SUBS == iota((size, size), 1) % SUBS
    return jnp.where(same, full, 0.0).astype(bf16)


def forces_kernel(
    modes,
    nodes,
    des,
    elems,
    conn_hbm,
    owner_hbm,
    mass_hbm,
    stiff_hbm,
    ref_hbm,
    eig_hbm,
    weight_hbm,
    own_hbm,
    field,
    low_ref,
    high_ref,
    resid_ref,
    power_ref,
    node_ref,
    conn,
    owner_row,
    eig_row,
    weight_row,
    owner_flat,
    mass_flat,
    stiff,
    ref,
    own,
    sems,
    stiff_sems,
    mass_row,
    dir_row,
    mass_big,
    hot,
    shapes,
    mass_q,
    stiff_wide,
    force,
    sums_t,
):
    rows = COMPS * modes
    tiles = elems // TILE
    rank = lax.axis_index("dom")
    mode_start = lax.axis_index("mode") * modes
    entries = 16
    small = [
        pltpu.make_async_copy(source, target, sems.at[i])
        for i, (source, target) in enumerate(
            (
                (ref_hbm, ref),
                (conn_hbm, conn),
                (owner_hbm, owner_flat),
                (mass_hbm, mass_flat),
                (eig_hbm, eig_row),
                (weight_hbm, weight_row),
                (own_hbm.at[pl.ds(rows, EXTRA)], own),
            )
        )
    ]

    def stiff_copy(t):
        cols = pl.ds(t * TILE, TILE)
        return pltpu.make_async_copy(stiff_hbm.at[:, :, cols], stiff.at[t], stiff_sems.at[t])

    for copy in small:
        copy.start()
    for t in range(tiles):
        stiff_copy(t).start()

    sums_t[...] = jnp.zeros_like(sums_t)
    for copy in small:
        copy.wait()
    per = des // LANES
    sides = []
    for pieces in (low_ref[rows : rows + EXTRA, :], own[...], high_ref[rows : rows + EXTRA, :]):
        packed = pieces.astype(f32)
        sides.append(packed[:per] + packed[per : 2 * per] + packed[2 * per : 3 * per])
    sides.append(jnp.zeros((entries - 3 * per, LANES), f32))
    table = jnp.concatenate(three_pieces(jnp.concatenate(sides, axis=0)), axis=0)
    mass_big[...] = expand_mass(ref[...])
    rows_of(owner_flat, owner_row)
    rows_of(mass_flat, mass_row)
    eig = column_of(eig_row[...], mode_start, modes)
    weight = 2.0 * column_of(weight_row[...], 0, modes)
    local = owner_row[...] - (rank - 1) * des
    looked = dot(table, one_hot(LANES, local % LANES))
    looked = looked[:entries] + looked[entries : 2 * entries] + looked[2 * entries :]
    here = iota((entries, elems), 0) == local // LANES
    dir_row[...] = jnp.sum(jnp.where(here, looked, 0.0), axis=0, keepdims=True)

    for t in range(tiles):
        at = t * TILE
        elem_dir = dir_row[:, pl.ds(at, TILE)]
        elem_mass = mass_row[:, pl.ds(at, TILE)]
        fill_one_hot(conn, at, hot, nodes)
        shapes[...] = dot(field[...], hot[...])
        for g in range(modes // SUBS):
            stacked = [
                shapes[
                    (b // CORNERS) * modes + g * SUBS : (b // CORNERS) * modes + (g + 1) * SUBS,
                    (b % CORNERS) * TILE : (b % CORNERS + 1) * TILE,
                ]
                for b in range(DOFS)
            ]
            mass_q[g] = dot(mass_big[...], jnp.concatenate(stacked, axis=0).astype(bf16))
        stiff_copy(t).wait()
        stiff_wide[...] = stiff[t].astype(f32)

        for lane in range(TILE // LANES):
            cols = slice(lane * LANES, (lane + 1) * LANES)
            at_lane = at + lane * LANES
            direction = elem_dir[:, cols]
            mass = elem_mass[:, cols]
            scaled = eig * mass
            dir_mass = direction * mass
            power = jnp.zeros((modes, LANES), f32)
            for first in range(0, DOFS, 4):
                sums = [jnp.zeros((modes, LANES), f32) for _ in range(4)]
                for b in range(DOFS):
                    c, k = b // CORNERS, b % CORNERS
                    col = k * TILE + lane * LANES
                    s = shapes[c * modes : (c + 1) * modes, col : col + LANES]
                    for q in range(4):
                        sums[q] = sums[q] + stiff_wide[first + q, b : b + 1, cols] * s
                for q in range(4):
                    c, k = (first + q) // CORNERS, (first + q) % CORNERS
                    col = k * TILE + lane * LANES
                    s = shapes[c * modes : (c + 1) * modes, col : col + LANES]
                    base = k * rows + c * modes
                    mq = jnp.concatenate(
                        [
                            mass_q[g, (first + q) * SUBS : (first + q + 1) * SUBS, cols]
                            for g in range(modes // SUBS)
                        ],
                        axis=0,
                    )
                    power = power + s * mq
                    span = slice(c * modes, (c + 1) * modes)
                    force[span, col : col + LANES] = (direction * sums[q]).astype(bf16)
                    span = slice(rows + c * modes, rows + (c + 1) * modes)
                    force[span, col : col + LANES] = (dir_mass * mq).astype(bf16)
                    resid_ref[base : base + modes, pl.ds(at_lane, LANES)] = weight * (
                        sums[q] - scaled * mq
                    )
            power_ref[:, pl.ds(at_lane, LANES)] = power * mass

        sums_t[...] += dot_nt(hot[...], force[...])

    for i in range((nodes + LANES) // LANES):
        span = slice(i * LANES, (i + 1) * LANES)
        for part in range(2 * rows // LANES):
            node_ref[part * LANES : (part + 1) * LANES, span] = sums_t[
                span, part * LANES : (part + 1) * LANES
            ].T


def gather_modes(refs, c, modes):
    return jnp.concatenate([r[c * modes : (c + 1) * modes, :] for r in refs], axis=0)


def gram_kernel(modes, groups, node_ref, eig_ref, *refs):
    fields, out_ref = refs[:groups], refs[groups]
    rows = COMPS * modes
    eig = column_of(eig_ref[...], lax.axis_index("mode") * modes, modes)
    grams = [jnp.zeros((modes, groups * modes), f32) for _ in range(2)]
    for c in range(COMPS):
        pieces = []
        for kind in range(2):
            base = kind * rows + c * modes
            pieces += three_pieces(node_ref[base : base + modes, :])
        each = dot_nt(jnp.concatenate(pieces, axis=0), gather_modes(fields, c, modes))
        each = [each[i * modes : (i + 1) * modes] for i in range(6)]
        grams = [grams[k] + (each[3 * k] + (each[3 * k + 1] + each[3 * k + 2])) for k in range(2)]
    stiff_gram, mass_gram = grams
    out_ref[0:modes, :] = stiff_gram - eig * mass_gram
    mask = iota(mass_gram.shape, 0) == iota(mass_gram.shape, 1)
    out_ref[modes : modes + 8, :] = jnp.broadcast_to(
        jnp.sum(jnp.where(mask, mass_gram, 0.0), axis=0, keepdims=True), (8, LANES)
    )


def energy_kernel(modes, groups, nodes, des, elems, gram_ref, eig_ref, weight_ref, *refs):
    fields, refs = refs[:groups], refs[groups:]
    conn_ref, owner_row, resid_ref, power_ref = refs[:4]
    low_ref, own_ref, high_ref, deriv_ref = refs[4:8]
    deriv, factor, hot, totals = refs[8:]
    rows = COMPS * modes
    rank = lax.axis_index("dom")
    mode_start = lax.axis_index("mode") * modes

    total = gram_ref[0]
    for i in range(1, gram_ref.shape[0]):
        total = total + gram_ref[i]
    gram = total[:modes]
    mass_diag = column_of(total[modes : modes + 1], 0, modes)
    shape = (modes, groups * modes)
    mask = iota(shape, 0) == iota(shape, 1)
    eig_rows = jnp.broadcast_to(eig_ref[...], (8, LANES))
    turned = pltpu.roll(eig_rows, lax.rem(LANES - mode_start, LANES), 1)[0:1]
    spacing = column_of(turned, 0, modes) - turned
    combiner = jnp.where(mask, -0.5 * mass_diag, gram / jnp.where(mask, 1.0, spacing)).astype(bf16)
    diagonal = jnp.where(mask, gram, 0.0)
    deriv_ref[...] = jnp.sum(diagonal, axis=0, keepdims=True)[:, :modes]
    eig_deriv = jnp.sum(diagonal, axis=1, keepdims=True)
    factor[...] = jnp.broadcast_to(eig_deriv * column_of(weight_ref[...], 0, modes), factor.shape)
    for c in range(COMPS):
        span = slice(c * modes, (c + 1) * modes)
        deriv[span, :] = dot(combiner, gather_modes(fields, c, modes)).astype(bf16)
    totals[...] = jnp.zeros_like(totals)

    for t in range(elems // TILE):
        at = t * TILE
        fill_one_hot(conn_ref, at, hot, nodes)
        moved = dot(deriv[...], hot[...])
        energies = []
        for lane in range(TILE // LANES):
            cols = pl.ds(at + lane * LANES, LANES)
            total = -factor[...] * power_ref[:, cols]
            for k in range(CORNERS):
                col = k * TILE + lane * LANES
                for c in range(COMPS):
                    base = k * rows + c * modes
                    total = total + moved[
                        c * modes : (c + 1) * modes, col : col + LANES
                    ] * resid_ref[base : base + modes, cols]
            energies.append(jnp.sum(total, axis=0, keepdims=True))
        energy = jnp.concatenate(energies, axis=1)
        local = owner_row[:, pl.ds(at, TILE)] - (rank - 1) * des
        entries = totals.shape[0]
        here = iota((entries, TILE), 0) == local // LANES
        spread = jnp.concatenate(
            [jnp.where(here, p.astype(f32), 0.0).astype(bf16) for p in three_pieces(energy)], axis=0
        )
        sums = dot_nt(spread, one_hot(LANES, local % LANES))
        totals[...] += sums[:entries] + sums[entries : 2 * entries] + sums[2 * entries :]

    per = des // LANES
    for side, ref in enumerate((low_ref, own_ref, high_ref)):
        for i in range(per):
            at = side * per + i
            ref[:, i * LANES : (i + 1) * LANES] = totals[at : at + 1, :]


def neighbour(value, step):
    count = lax.axis_size("dom")
    pairs = [(i, i + step) for i in range(count) if 0 <= i + step < count]
    return lax.ppermute(value, "dom", pairs)


def shift_in(value, axis, step):
    count = lax.axis_size(axis)
    return lax.ppermute(value, axis, [(i, (i - step) % count) for i in range(count)])


def from_all(value, axis, groups):
    size = len(groups[0])
    copies = jnp.broadcast_to(value[None], (size,) + value.shape)
    return lax.all_to_all(copies, axis, 0, 0, axis_index_groups=groups)


def whole(shape):
    return pl.BlockSpec(shape, lambda t: (0,) * len(shape))


def params(mib):
    return pltpu.CompilerParams(vmem_limit_bytes=mib * MIB)


def cost(flops, bytes_):
    return pl.CostEstimate(flops=flops, bytes_accessed=bytes_, transcendentals=0)


def on_device(
    mode_shapes,
    eigenvalues,
    mode_weights,
    stiff_deriv,
    mass_ref,
    mass_scale,
    connectivity,
    design_owner,
    direction,
):
    modes, _, nodes = mode_shapes.shape
    elems = connectivity.shape[1]
    des = direction.shape[0]
    groups = lax.axis_size("mode")
    count = lax.axis_size("dom")
    total_modes = groups * modes
    rows = COMPS * modes
    big = CORNERS * rows
    tiles = elems // TILE
    wide = CORNERS * TILE
    entries = 16
    shaped = jax.ShapeDtypeStruct
    vmem = pl.BlockSpec(memory_space=pltpu.VMEM)
    hbm = pl.BlockSpec(memory_space=pltpu.HBM)

    field = jnp.transpose(mode_shapes, (1, 0, 2)).reshape(rows, nodes)
    eig_row = eigenvalues.reshape(1, total_modes)
    weight_row = mode_weights.reshape(1, modes)

    up, down = pl.pallas_call(
        functools.partial(pack_kernel, rows, des),
        grid=(1,),
        in_specs=[
            pl.BlockSpec((rows, LANES), lambda t: (0, 0)),
            pl.BlockSpec((rows, LANES), lambda t: (0, nodes // LANES - 1)),
            whole((des,)),
        ],
        out_specs=[whole((rows + EXTRA, LANES))] * 2,
        out_shape=[shaped((rows + EXTRA, LANES), bf16)] * 2,
        name="pack",
    )(field, field, direction)
    low, high = neighbour(up, 1), neighbour(down, -1)
    upper = lax.broadcasted_iota(jnp.int32, (rows, LANES), 1) < LANES // 2
    extended = jnp.concatenate([field, jnp.where(upper, high[:rows], low[:rows])], axis=1)
    fields = [extended] + [shift_in(extended, "mode", s) for s in range(1, groups)]

    def pinned(*values):
        return [pltpu.with_memory_space_constraint(v, pltpu.HBM) for v in values]

    resid, power, node, conn, owner_row, eig_copy, weight_copy = pl.pallas_call(
        functools.partial(forces_kernel, modes, nodes, des, elems),
        in_specs=[hbm] * 8 + [vmem] * 3,
        out_specs=[vmem] * 7,
        out_shape=[
            shaped((big, elems), f32),
            shaped((modes, elems), f32),
            shaped((2 * rows, nodes + LANES), f32),
            shaped((CORNERS, elems), jnp.int32),
            shaped((1, elems), jnp.int32),
            shaped((1, total_modes), f32),
            shaped((1, modes), f32),
        ],
        scratch_shapes=[
            pltpu.VMEM((elems,), jnp.int32),
            pltpu.VMEM((elems,), f32),
            pltpu.VMEM((tiles, DOFS, DOFS, TILE), bf16),
            pltpu.VMEM((DOFS, DOFS), bf16),
            pltpu.VMEM((EXTRA, LANES), bf16),
            pltpu.SemaphoreType.DMA((7,)),
            pltpu.SemaphoreType.DMA((tiles,)),
            pltpu.VMEM((1, elems), f32),
            pltpu.VMEM((1, elems), f32),
            pltpu.VMEM((DOFS * SUBS, DOFS * SUBS), bf16),
            pltpu.VMEM((nodes + LANES, wide), bf16),
            pltpu.VMEM((rows, wide), f32),
            pltpu.VMEM((modes // SUBS, DOFS * SUBS, TILE), f32),
            pltpu.VMEM((DOFS, DOFS, TILE), f32),
            pltpu.VMEM((2 * rows, wide), bf16),
            pltpu.VMEM((nodes + LANES, 2 * rows), f32),
        ],
        compiler_params=params(44),
        cost_estimate=cost(1_000_000, 100_000),
        name="forces",
    )(
        *pinned(
            connectivity,
            design_owner,
            mass_scale,
            stiff_deriv,
            mass_ref,
            eig_row,
            weight_row,
            up,
        ),
        extended,
        low,
        high,
    )

    gram = pl.pallas_call(
        functools.partial(gram_kernel, modes, groups),
        out_shape=shaped((modes + 8, total_modes), f32),
        compiler_params=params(24),
        name="gram",
    )(node, eig_copy, *fields)

    gram = gram + lax.ppermute(gram, "dom", [(i, i ^ 1) for i in range(count)])
    grams = from_all(gram, "dom", [list(range(core, count, 2)) for core in range(2)])

    low_sum, own_sum, high_sum, eig_deriv = pl.pallas_call(
        functools.partial(energy_kernel, modes, groups, nodes, des, elems),
        in_specs=[vmem] * (7 + groups),
        out_specs=[vmem] * 4,
        out_shape=[shaped((1, des), f32)] * 3 + [shaped((1, modes), f32)],
        scratch_shapes=[
            pltpu.VMEM((rows, nodes + LANES), bf16),
            pltpu.VMEM((modes, LANES), f32),
            pltpu.VMEM((nodes + LANES, wide), bf16),
            pltpu.VMEM((entries, LANES), f32),
        ],
        compiler_params=params(44),
        name="energy",
    )(grams, eig_copy, weight_copy, *fields, conn, owner_row, resid, power)

    owned = own_sum + neighbour(low_sum, -1) + neighbour(high_sum, 1)
    hess_vec = jnp.sum(from_all(owned, "mode", [list(range(groups))]), axis=0)
    return (hess_vec.reshape(des), eig_deriv.reshape(modes))


def solution(mesh):
    return jax.shard_map(
        on_device,
        mesh=mesh,
        in_specs=(
            P("mode", None, "dom"),
            P(),
            P("mode"),
            P(None, None, "dom"),
            P(),
            P("dom"),
            P(None, "dom"),
            P("dom"),
            P("dom"),
        ),
        out_specs=(P("dom"), P("mode")),
        check_vma=False,
    )
```
